512 devices in a mesh: frames: 128 (over z, y, core), heads: 4 (over x).
Axes of the slice: x: 4, y: 8, z: 8, core: 2. Of those that a mesh axis runs over, the one named last changes fastest.
Arguments:
- activations: bfloat16 [16384, 2048], P('frames', 'heads'), may hold values from -6 to 6
- norm_gain: bfloat16 [2048], P('heads'), may hold values from 0.099609375 to 1.8984375
- w_query: bfloat16 [2048, 2048], P('frames', 'heads'), may hold values from -0.125 to 0.125
- w_key: bfloat16 [2048, 2048], P('frames', 'heads'), may hold values from -0.125 to 0.125
- w_value: bfloat16 [2048, 2048], P('frames', 'heads'), may hold values from -0.125 to 0.125
- out_grad: bfloat16 [16384, 2048], P('frames', 'heads'), may hold values from -6 to 6
Outputs:
- input_grad: bfloat16 [16384, 2048], P('frames', 'heads')
- gain_grad: float32 [2048], P('heads')
The draws below stay inside these ranges and needn't reach their ends.
All inputs are finite; a program needn't handle non-finite values.
Results may differ from the reference program's by a relative error of at most 0.009.
Values may be sent and summed in bfloat16 or wider, within the bound.
A program may use at most 64 MiB of HBM per device.

```python
import jax
import jax.numpy as jnp
from jax import lax

D = 2048
HEADS = 16
HDIM = 128
POS = 128
INNER = 2048
FRAMES = 128
TOKENS = 16384


def levels(own_key, dims, cuts, low, top_value):
    factor_of = 1.0
    for position, shards_of in cuts:
        draws = jax.random.uniform(jax.random.fold_in(jax.random.fold_in(own_key, 6), position), (shards_of,), jnp.float32, low / len(cuts), top_value / len(cuts))
        factor_of = factor_of * jnp.repeat(jnp.exp(draws), dims[position] // shards_of).reshape((-1,) + (1,) * (len(dims) - 1 - position))
    return factor_of


def gaussian(key, extent, spread, limit, split=(), kind=jnp.bfloat16):
    array = jax.random.normal(key, extent, jnp.float32) * spread
    if len(split) > 0:
        array = levels(key, extent, split, -0.22, 0.18) * array
    return jnp.clip(array, min=-limit, max=limit).astype(kind)


def setup_inputs(seed: int = 0) -> dict:
    key_of = jax.random.split(jax.random.key(seed), 7)
    activations = gaussian(key_of[0], (TOKENS, D), 1.0, 6.0, ((0, 128), (1, 4)))
    norm_gain = jnp.clip(1.0 + 0.18 * jax.random.normal(key_of[1], (D,), jnp.float32), 0.099609375, 1.8984375).astype(jnp.bfloat16)
    w_query = gaussian(key_of[2], (D, INNER), D ** -0.5, 0.125, ((0, 128), (1, 4)))
    w_key = gaussian(key_of[3], (D, INNER), D ** -0.5, 0.125, ((0, 128), (1, 4)))
    w_value = gaussian(key_of[4], (D, INNER), D ** -0.5, 0.125, ((0, 128), (1, 4)))
    out_grad = gaussian(key_of[5], (TOKENS, INNER), 1.0, 6.0, ((0, 128), (1, 4)))
    return dict(activations=activations, norm_gain=norm_gain, w_query=w_query, w_key=w_key, w_value=w_value, out_grad=out_grad)


EPS = 1e-05

def head_backward(operands):
    queries, key_rows, value_rows, grad_rows = operands
    score_scale = HDIM ** (-0.5)
    queries = queries.astype(jnp.float32)
    key_rows = key_rows.astype(jnp.float32)
    value_rows = value_rows.astype(jnp.float32)
    grad_rows = grad_rows.astype(jnp.float32)
    scores = jnp.einsum('tpd,upd->ptu', queries, key_rows) * score_scale
    later_idx = lax.broadcasted_iota(jnp.int32, (FRAMES, FRAMES), 0)
    earlier_idx = lax.broadcasted_iota(jnp.int32, (FRAMES, FRAMES), 1)
    causal = later_idx >= earlier_idx
    exp_scores = jnp.where(causal, jnp.exp(jnp.where(causal, scores, 0.0)), 0.0)
    weights = exp_scores / lax.optimization_barrier(jnp.sum(exp_scores, axis=-1, keepdims=True))
    weights_low = weights.astype(jnp.bfloat16).astype(jnp.float32)
    dweights = jnp.einsum('tpd,upd->ptu', grad_rows, value_rows)
    row_delta = lax.optimization_barrier(jnp.sum(weights * dweights, axis=-1, keepdims=True))
    dscores = (weights * (dweights - row_delta) * score_scale).astype(jnp.bfloat16).astype(jnp.float32)
    dquery = jnp.einsum('ptu,upd->tpd', dscores, key_rows).astype(jnp.bfloat16)
    dkey = jnp.einsum('ptu,tpd->upd', dscores, queries).astype(jnp.bfloat16)
    dvalue = jnp.einsum('ptu,tpd->upd', weights_low, grad_rows).astype(jnp.bfloat16)
    return (dquery, dkey, dvalue)

def split_heads(matrix):
    return matrix.reshape(FRAMES, POS, HEADS, HDIM).transpose(2, 0, 1, 3)

def join_heads(stacked):
    return stacked.transpose(1, 2, 0, 3).reshape(TOKENS, INNER)

def reference(activations, norm_gain, w_query, w_key, w_value, out_grad):
    values_f = activations.astype(jnp.float32)
    gain_f = norm_gain.astype(jnp.float32)
    inverse_rms = lax.rsqrt(lax.optimization_barrier(jnp.sum(values_f * values_f, axis=1, keepdims=True)) / D + EPS)
    normed = (values_f * inverse_rms * gain_f).astype(jnp.bfloat16)
    queries = jnp.dot(normed, w_query, preferred_element_type=jnp.float32).astype(jnp.bfloat16)
    key_rows = jnp.dot(normed, w_key, preferred_element_type=jnp.float32).astype(jnp.bfloat16)
    value_rows = jnp.dot(normed, w_value, preferred_element_type=jnp.float32).astype(jnp.bfloat16)
    dquery, dkey, dvalue = lax.map(head_backward, (split_heads(queries), split_heads(key_rows), split_heads(value_rows), split_heads(out_grad)))
    grad_normed = jnp.dot(join_heads(dquery), w_query.T, preferred_element_type=jnp.float32)
    grad_normed = grad_normed + jnp.dot(join_heads(dkey), w_key.T, preferred_element_type=jnp.float32)
    grad_normed = grad_normed + jnp.dot(join_heads(dvalue), w_value.T, preferred_element_type=jnp.float32)
    gain_grad = lax.optimization_barrier(jnp.sum(grad_normed * values_f * inverse_rms, axis=0))
    scaled = grad_normed * gain_f
    products = lax.optimization_barrier(jnp.sum(scaled * values_f, axis=1, keepdims=True))
    input_grad = (inverse_rms * scaled - values_f * inverse_rms ** 3 * products / D).astype(jnp.bfloat16)
    return (input_grad, gain_grad)
```

```python
import functools

import jax
import jax.numpy as jnp
from jax import lax
from jax.experimental import pallas as pl
from jax.experimental.pallas import tpu as pltpu
from jax.sharding import PartitionSpec as P

EPS = 1e-05
HDIM = 128
F32 = jnp.float32
BF16 = jnp.bfloat16
NT = (((1,), (1,)), ((), ()))
TN = (((0,), (0,)), ((), ()))


def dot(a, b, dims=(((1,), (0,)), ((), ()))):
    return lax.dot_general(a, b, dims, preferred_element_type=F32)


def kernel(
    nz, ny, nx,
    a_ref, gain_ref, wq_ref, wk_ref, wv_ref, og_ref,
    out_ref, gg_ref,
    w0, w1, stage, za, zg, sa, sg, xf, nrm, ogf, gmix,
    gains, gsum, gpart, gx, gy, gz, gsend, ig, part, xsend, xrecv, ysend, yrecv, zsend, zrecv,
    w_s, w_r, p1_s, p1_r, p2_s, p2_r, az_s, az_r, ay_s, ay_r, ax_s, ax_r, ac_s, ac_r,
    oc_s, oc_r, gn_s, gn_r, pr_s, pr_r, xs_s, xs_r, gp_s, gp_r, gx_s, gx_r, gy_s, gy_r, gz_s, gz_r,
    oy_s, oy_r, oz_s, oz_r,
):
    frame = lax.axis_index("frames")
    x = lax.axis_index("heads")
    c = lax.rem(frame, 2)
    y = lax.rem(lax.div(frame, 2), ny)
    z = lax.div(frame, 2 * ny)
    chip = z * ny + y
    width = a_ref.shape[1]
    model = width * nx
    tokens = 2 * nz * ny
    zrows = 2 * ny
    yrows = 2 * nz
    wrows = wq_ref.shape[0]
    crows = 2 * wrows
    ws = (w0, w1)

    def dev(z_, y_, c_, x_):
        return ((z_ * ny + y_) * 2 + c_, x_)

    def rcopy(src, dst, ssem, rsem, to):
        return pltpu.make_async_remote_copy(
            src_ref=src, dst_ref=dst, send_sem=ssem, recv_sem=rsem,
            device_id=to, device_id_type=pl.DeviceIdType.MESH,
        )

    def wrap(v, n):
        return lax.rem(v + 2 * n, n)

    def mult(v, m):
        return pl.multiple_of(v * m, m)

    mate = dev(z, y, 1 - c, x)
    own_rows = pl.ds(mult(c, tokens), tokens)
    mate_rows = pl.ds(mult(1 - c, tokens), tokens)

    def yp(o):
        return wrap(y + o, ny)

    def zp(o):
        return wrap(z + o, nz)

    def xp(o):
        return wrap(x + o, nx)

    bar = pltpu.get_barrier_semaphore()

    def hello(to):
        pl.semaphore_signal(bar, inc=1, device_id=to, device_id_type=pl.DeviceIdType.MESH)

    hello(mate)
    for o in range(1, ny):
        hello(dev(z, yp(o), c, x))
    for o in range(1, nz):
        hello(dev(zp(o), y, c, x))
    for o in range(1, nx):
        hello(dev(z, y, c, xp(o)))
    pl.semaphore_wait(bar, 1 + (ny - 1) + (nz - 1) + (nx - 1))

    def z_send(src, dst, s, r):
        def copy(o):
            to = zp(o)
            return rcopy(
                src.at[pl.ds(mult(to, zrows), zrows)], dst.at[pl.ds(mult(z, zrows), zrows)],
                s.at[to], r.at[z], dev(to, y, c, x),
            )
        return copy

    def z_wait(dst, s, r, o):
        at = zp(o)
        ref = dst.at[pl.ds(mult(at, zrows), zrows)]
        rcopy(ref, ref, s.at[at], r.at[at], dev(at, y, c, x)).wait_recv()

    def y_send(src, dst, dst_base, dst_cols, s, r):
        def copy(o):
            to = yp(o)
            return rcopy(
                src.at[pl.ds(mult(to, yrows), yrows)],
                dst.at[pl.ds(pl.multiple_of(dst_base + y * yrows, yrows), yrows), dst_cols],
                s.at[to], r.at[y], dev(z, to, c, x),
            )
        return copy

    def y_wait(dst, dst_base, dst_cols, s, r, o):
        at = yp(o)
        ref = dst.at[pl.ds(pl.multiple_of(dst_base + at * yrows, yrows), yrows), dst_cols]
        rcopy(ref, ref, s.at[at], r.at[at], dev(z, at, c, x)).wait_recv()

    def swapped(value, na, nb):
        i = lax.broadcasted_iota(jnp.int32, (tokens, tokens), 0)
        j = lax.broadcasted_iota(jnp.int32, (tokens, tokens), 1)
        b = lax.div(i, 2 * na)
        a = lax.rem(lax.div(i, 2), na)
        pair = lax.rem(i, 2)
        hot = jnp.where(j == (a * nb + b) * 2 + pair, 1.0, 0.0).astype(BF16)
        return dot(hot, value).astype(BF16)

    own_cols = pl.ds(mult(x, width), width)
    all_cols = pl.ds(0, width)

    az = z_send(a_ref, za, az_s, az_r)
    for o in range(1, nz):
        az(o).start()

    for j in range(2):
        for i, w_ref in enumerate((wq_ref, wk_ref, wv_ref)):
            mine = pl.ds(mult(2 * c + j, HDIM), HDIM)
            theirs = pl.ds(mult(2 * (1 - c) + j, HDIM), HDIM)
            ws[j][pl.ds(pl.multiple_of(chip * crows + c * wrows, wrows), wrows), i * HDIM:(i + 1) * HDIM] = w_ref[:, mine]
            stage[j, :, i * HDIM:(i + 1) * HDIM] = w_ref[:, theirs]

    def w_mate(j, core):
        return rcopy(
            stage.at[j], ws[j].at[pl.ds(pl.multiple_of(chip * crows + core * wrows, wrows), wrows)],
            w_s.at[j], w_r.at[j], mate,
        )

    for j in range(2):
        w_mate(j, c).start()

    gains[x] = gain_ref[...].astype(F32)

    def gain_copy(o):
        return rcopy(gains.at[x], gains.at[x], gn_s.at[xp(o)], gn_r.at[x], dev(z, y, c, xp(o)))

    for o in range(1, nx):
        gain_copy(o).start()

    def block(zb, yb):
        return pl.ds(mult(zb * ny + yb, crows), crows)

    def p1(j, o):
        ref = ws[j].at[block(z, y)]
        to = dev(z, yp(o), c, x) if j == 0 else dev(zp(o), y, c, x)
        return rcopy(ref, ref, p1_s.at[j, o], p1_r.at[j, o], to)

    def p1_wait(j, o):
        ref = ws[j].at[block(z, yp(-o)) if j == 0 else block(zp(-o), y)]
        rcopy(ref, ref, p1_s.at[j, o], p1_r.at[j, o], mate).wait_recv()

    def place(j, d, age, k):
        sign = 1 if d == 0 else -1
        if j == 0:
            return ws[0].at[block(zp(-sign * age), wrap(y - k, ny))]
        return ws[1].at[block(wrap(z - k, nz), yp(-sign * age))]

    def p2(j, d, age, k):
        sign = 1 if d == 0 else -1
        to = dev(zp(sign), y, c, x) if j == 0 else dev(z, yp(sign), c, x)
        ref = place(j, d, age, k)
        return rcopy(ref, ref, p2_s.at[j, d, age, k], p2_r.at[j, d, age, k], to)

    def p2_wait(j, d, age, k):
        ref = place(j, d, age + 1, k)
        rcopy(ref, ref, p2_s.at[j, d, age, k], p2_r.at[j, d, age, k], mate).wait_recv()

    ring = nz
    subs = ny
    last = ring // 2 - 1

    def goes(d, age, k):
        if age < last:
            return True
        if age > last:
            return False
        return (k < subs // 2) if d == 0 else (k >= subs // 2)

    for j in range(2):
        w_mate(j, 1 - c).wait_recv()
    for d in range(2):
        if goes(d, 0, 0):
            for j in range(2):
                p2(j, d, 0, 0).start()
    order = sorted(range(1, ny), key=lambda o: min(o, ny - o))
    for o in order:
        for j in range(2):
            p1(j, o).start()

    za[pl.ds(mult(z, zrows), zrows), :] = a_ref[pl.ds(mult(z, zrows), zrows), :]
    for o in range(1, nz):
        z_wait(za, az_s, az_r, o)
    sa[...] = swapped(za[...], nz, ny)
    ay = y_send(sa, xf, c * tokens, own_cols, ay_s, ay_r)
    for o in range(1, ny):
        ay(o).start()
    xf[pl.ds(pl.multiple_of(c * tokens + y * yrows, yrows), yrows), own_cols] = sa[pl.ds(mult(y, yrows), yrows), :]

    for k in order:
        for j in range(2):
            p1_wait(j, k)
            for d in range(2):
                if goes(d, 0, k):
                    p2(j, d, 0, k).start()

    for o in range(1, ny):
        y_wait(xf, c * tokens, own_cols, ay_s, ay_r, o)

    def xcols(at):
        return pl.ds(mult(at, width), width)

    def ax(o):
        ref = xf.at[own_rows, own_cols]
        return rcopy(ref, ref, ax_s.at[xp(o)], ax_r.at[x], dev(z, y, c, xp(o)))

    def ac(at):
        ref = xf.at[own_rows, xcols(at)]
        return rcopy(ref, ref, ac_s.at[at], ac_r.at[at], mate)

    for o in (2, 1, 3)[-(nx - 1):] if nx == 4 else range(1, nx):
        ax(o).start()
    ac(x).start()

    oz = z_send(og_ref, zg, oz_s.at[0], oz_r.at[0])
    for o in range(1, nz):
        oz(o).start()

    def hop(age):
        @pl.loop(0, subs // 2)
        def _(k):
            for j in range(2):
                for d in range(2):
                    p2_wait(j, d, age - 1, k)
                    if goes(d, age, 0):
                        p2(j, d, age, k).start()

        @pl.loop(subs // 2, subs)
        def _(k):
            for j in range(2):
                for d in range(2):
                    p2_wait(j, d, age - 1, k)
                    if goes(d, age, subs - 1):
                        p2(j, d, age, k).start()

    if last >= 1:
        hop(1)

    zg[pl.ds(mult(z, zrows), zrows), :] = og_ref[pl.ds(mult(z, zrows), zrows), :]
    for o in range(1, nz):
        z_wait(zg, oz_s.at[0], oz_r.at[0], o)
    sg[0] = swapped(zg[...], nz, ny)
    oy = y_send(sg.at[0], sg.at[1], 0, all_cols, oy_s.at[0], oy_r.at[0])
    for o in range(1, ny):
        oy(o).start()
    sg[1, pl.ds(mult(y, yrows), yrows), :] = sg[0, pl.ds(mult(y, yrows), yrows), :]

    for o in range(1, nx):
        at = xp(o)
        ref = xf.at[own_rows, xcols(at)]
        rcopy(ref, ref, ax_s.at[at], ax_r.at[at], mate).wait_recv()
        ac(at).start()

    if last >= 2:
        hop(2)

    for o in range(1, ny):
        y_wait(sg.at[1], 0, all_cols, oy_s.at[0], oy_r.at[0], o)

    def oc(core):
        cols = pl.ds(mult(1 - core, 2 * HDIM), 2 * HDIM)
        return rcopy(
            sg.at[1, :, cols], ogf.at[pl.ds(mult(core, tokens), tokens)], oc_s, oc_r, mate,
        )

    oc(c).start()
    ogf[own_rows, :] = sg[1, :, pl.ds(mult(c, 2 * HDIM), 2 * HDIM)]

    for at in range(nx):
        ref = xf.at[mate_rows, at * width:(at + 1) * width]
        rcopy(ref, ref, ac_s.at[at], ac_r.at[at], mate).wait_recv()
    for o in range(1, nx):
        at = xp(o)
        rcopy(gains.at[at], gains.at[at], gn_s.at[at], gn_r.at[at], mate).wait_recv()
    square_sum = jnp.zeros((2 * tokens, 1), F32)
    for at in range(nx):
        act = xf[:, at * width:(at + 1) * width].astype(F32)
        square_sum += jnp.sum(act * act, axis=1, keepdims=True)
    inverse_rms = lax.rsqrt(square_sum / model + EPS)
    for at in range(nx):
        act = xf[:, at * width:(at + 1) * width].astype(F32)
        nrm[:, at * width:(at + 1) * width] = (act * inverse_rms * gains[at]).astype(BF16)

    if last >= 3:
        hop(3)

    rcopy(sg.at[1, :, 0:2 * HDIM], ogf.at[mate_rows], oc_s, oc_r, mate).wait_recv()

    @pl.loop(0, subs // 2)
    def _(k):
        for j in range(2):
            p2_wait(j, 0, last, k)

    @pl.loop(subs // 2, subs)
    def _(k):
        for j in range(2):
            p2_wait(j, 1, last, k)

    i = lax.broadcasted_iota(jnp.int32, (2 * tokens, 1), 0)
    j = lax.broadcasted_iota(jnp.int32, (1, 2 * tokens), 1)

    def frame_of(r):
        core = lax.div(r, tokens)
        yy = lax.rem(lax.div(r, yrows), ny)
        zz = lax.rem(lax.div(r, 2), nz)
        return (zz * ny + yy) * 2 + core

    causal = (frame_of(i) >= frame_of(j)) & (lax.rem(i, 2) == lax.rem(j, 2))
    scale = HDIM ** (-0.5)
    inner = jnp.zeros((2 * tokens, 1), F32)
    for h in range(2):
        proj = dot(nrm[...], ws[h][...])
        low = proj.astype(BF16)
        q, k, v = low[:, :HDIM], low[:, HDIM:2 * HDIM], low[:, 2 * HDIM:]
        g = ogf[:, h * HDIM:(h + 1) * HDIM]
        scores = dot(q, k, NT) * scale
        exps = jnp.where(causal, jnp.exp(jnp.where(causal, scores, 0.0)), 0.0)
        probs = exps / jnp.sum(exps, axis=1, keepdims=True)
        dprobs = dot(g, v, NT)
        delta = jnp.sum(probs * dprobs, axis=1, keepdims=True)
        dscores = (probs * (dprobs - delta) * scale).astype(BF16)
        gq = dot(dscores, k).astype(BF16)
        gk = dot(dscores, q, TN).astype(BF16)
        gv = dot(probs.astype(BF16), g, TN).astype(BF16)
        for n, part_of in enumerate((gq, gk, gv)):
            gmix[h, :, n * HDIM:(n + 1) * HDIM] = part_of
            inner += jnp.sum(part_of.astype(F32) * proj[:, n * HDIM:(n + 1) * HDIM], axis=1, keepdims=True)
    inner = inner / model

    xorder = (2, 1, 3, 0) if nx == 4 else tuple(range(1, nx)) + (0,)

    def pr(b, core):
        return rcopy(
            ig.at[b, pl.ds(mult(1 - core, tokens), tokens)], part.at[b], pr_s.at[b], pr_r.at[b], mate,
        )

    def xs(b, o):
        return rcopy(xsend.at[b], xrecv.at[b], xs_s.at[b], xs_r.at[b], dev(z, y, c, xp(o)))

    def forward(b):
        pr(b, 1 - c).wait_recv()
        total = ig[b, own_rows, :] + part[b]
        if b < nx - 1:
            xsend[b] = total.astype(BF16)
            xs(b, xorder[b]).start()
        else:
            ig[b, own_rows, :] = total

    for b, o in enumerate(xorder):
        at = xp(o)
        feats = pl.ds(mult(at, width), width)
        gn = dot(gmix[0], w0[feats, :], NT) + dot(gmix[1], w1[feats, :], NT)
        act = xf[:, feats].astype(F32) * inverse_rms
        gsum[at] = jnp.sum(gn * act, axis=0, keepdims=True)
        ig[b] = inverse_rms * (gn * gains[at] - act * inner)
        pr(b, c).start()
        if b > 0:
            forward(b - 1)
    gp = rcopy(gsum, gpart, gp_s, gp_r, mate)
    gp.start()
    forward(nx - 1)
    gp.wait_recv()
    gp.wait_send()
    gsum[...] += gpart[...]

    def gxc(o):
        return rcopy(gsum.at[xp(o)], gx.at[x], gx_s.at[xp(o)], gx_r.at[x], dev(z, y, c, xp(o)))

    for o in range(1, nx):
        gxc(o).start()
    gx[x] = gsum[x]

    total = ig[nx - 1, own_rows, :]
    for b in range(nx - 1):
        xs(b, xorder[b]).wait_recv()
        total += xrecv[b].astype(F32)
    ysend[...] = total.astype(BF16)
    by = y_send(ysend, yrecv, 0, all_cols, oy_s.at[1], oy_r.at[1])
    for o in range(1, ny):
        by(o).start()
    for o in range(1, nx):
        at = xp(o)
        rcopy(gx.at[at], gx.at[at], gx_s.at[at], gx_r.at[at], mate).wait_recv()
    gsend[0] = jnp.sum(gx[...], axis=0)
    gy[y] = gsend[0]

    def gyc(o):
        return rcopy(gsend.at[0], gy.at[y], gy_s.at[yp(o)], gy_r.at[y], dev(z, yp(o), c, x))

    def gzc(o):
        return rcopy(gsend.at[1], gz.at[z], gz_s.at[zp(o)], gz_r.at[z], dev(zp(o), y, c, x))

    for o in range(1, ny):
        gyc(o).start()
    yrecv[pl.ds(mult(y, yrows), yrows), :] = ysend[pl.ds(mult(y, yrows), yrows), :]
    for o in range(1, ny):
        y_wait(yrecv, 0, all_cols, oy_s.at[1], oy_r.at[1], o)
    zsend[...] = swapped(yrecv[...], ny, nz)
    bz = z_send(zsend, zrecv, oz_s.at[1], oz_r.at[1])
    for o in range(1, nz):
        bz(o).start()
    for o in range(1, ny):
        at = yp(o)
        rcopy(gy.at[at], gy.at[at], gy_s.at[at], gy_r.at[at], mate).wait_recv()
    gsend[1] = jnp.sum(gy[...], axis=0)
    gz[z] = gsend[1]
    for o in range(1, nz):
        gzc(o).start()
    zrecv[pl.ds(mult(z, zrows), zrows), :] = zsend[pl.ds(mult(z, zrows), zrows), :]

    for j in range(2):
        w_mate(j, c).wait_send()
        for o in range(1, ny):
            p1(j, o).wait_send()
    for age in range(last + 1):
        for half in range(2):
            @pl.loop(half * (subs // 2), (half + 1) * (subs // 2))
            def _(k):
                for j in range(2):
                    for d in range(2):
                        if goes(d, age, half * (subs - 1)):
                            p2(j, d, age, k).wait_send()
    for o in range(1, nz):
        az(o).wait_send()
        oz(o).wait_send()
    for o in range(1, ny):
        ay(o).wait_send()
        oy(o).wait_send()
        by(o).wait_send()
        gyc(o).wait_send()
    for o in range(1, nx):
        gain_copy(o).wait_send()
        ax(o).wait_send()
        gxc(o).wait_send()
    for at in range(nx):
        ac(at).wait_send()
    oc(c).wait_send()
    for b, o in enumerate(xorder):
        pr(b, c).wait_send()
        if b < nx - 1:
            xs(b, o).wait_send()

    for o in range(1, nz):
        z_wait(zrecv, oz_s.at[1], oz_r.at[1], o)
    out_ref[...] = zrecv[...]
    for o in range(1, nz):
        at = zp(o)
        rcopy(gz.at[at], gz.at[at], gz_s.at[at], gz_r.at[at], mate).wait_recv()
    gg_ref[...] = jnp.sum(gz[...], axis=0)
    for o in range(1, nz):
        bz(o).wait_send()
        gzc(o).wait_send()


def shards(nz, ny, nx, activations, norm_gain, w_query, w_key, w_value, out_grad):
    tokens, width = activations.shape
    model = width * nx
    wcols = 3 * HDIM
    wrows = w_query.shape[0]
    vmem = pl.BlockSpec(memory_space=pltpu.VMEM)
    dma = pltpu.SemaphoreType.DMA
    ring = nz // 2
    scratch = [
        pltpu.VMEM((model, wcols), BF16),
        pltpu.VMEM((model, wcols), BF16),
        pltpu.VMEM((2, wrows, wcols), BF16),
        pltpu.VMEM((tokens, width), BF16),
        pltpu.VMEM((tokens, width), BF16),
        pltpu.VMEM((tokens, width), BF16),
        pltpu.VMEM((2, tokens, width), BF16),
        pltpu.VMEM((2 * tokens, model), BF16),
        pltpu.VMEM((2 * tokens, model), BF16),
        pltpu.VMEM((2 * tokens, 2 * HDIM), BF16),
        pltpu.VMEM((2, 2 * tokens, wcols), BF16),
        pltpu.VMEM((nx, 1, width), F32),
        pltpu.VMEM((nx, 1, width), F32),
        pltpu.VMEM((nx, 1, width), F32),
        pltpu.VMEM((nx, 1, width), F32),
        pltpu.VMEM((ny, 1, width), F32),
        pltpu.VMEM((nz, 1, width), F32),
        pltpu.VMEM((2, 1, width), F32),
        pltpu.VMEM((nx, 2 * tokens, width), F32),
        pltpu.VMEM((nx, tokens, width), F32),
        pltpu.VMEM((nx, tokens, width), BF16),
        pltpu.VMEM((nx, tokens, width), BF16),
        pltpu.VMEM((tokens, width), BF16),
        pltpu.VMEM((tokens, width), BF16),
        pltpu.VMEM((tokens, width), BF16),
        pltpu.VMEM((tokens, width), BF16),
    ]
    for shape in (
        (2,), (2, ny), (2, 2, ring, ny), (nz,), (ny,), (nx,), (nx,),
        (), (nx,), (nx,), (nx,), (), (nx,), (ny,), (nz,),
        (2, ny), (2, nz),
    ):
        scratch += [dma(shape), dma(shape)] if shape else [dma, dma]
    out, gain = pl.pallas_call(
        functools.partial(kernel, nz, ny, nx),
        out_shape=(
            jax.ShapeDtypeStruct((tokens, width), BF16),
            jax.ShapeDtypeStruct((1, width), F32),
        ),
        in_specs=[vmem] * 6,
        out_specs=(vmem, vmem),
        scratch_shapes=scratch,
        compiler_params=pltpu.CompilerParams(
            collective_id=0, has_side_effects=True, vmem_limit_bytes=48 * 1024 * 1024
        ),
    )(activations, norm_gain.reshape(1, width), w_query, w_key, w_value, out_grad)
    return out, gain.reshape(width)


def solution(mesh, nz=8, ny=8):
    nx = mesh.shape["heads"]
    in_specs = (
        P("frames", "heads"),
        P("heads"),
        P("frames", "heads"),
        P("frames", "heads"),
        P("frames", "heads"),
        P("frames", "heads"),
    )
    out_specs = (P("frames", "heads"), P("heads"))
    return jax.shard_map(
        functools.partial(shards, nz, ny, nx),
        mesh=mesh, in_specs=in_specs, out_specs=out_specs, check_vma=False,
    )
```

```python
import functools

import jax
import jax.numpy as jnp
from jax import lax
from jax.experimental import pallas as pl
from jax.experimental.pallas import tpu as pltpu
from jax.sharding import PartitionSpec as P

EPS = 1e-05
HDIM = 128
F32 = jnp.float32
BF16 = jnp.bfloat16
NT = (((1,), (1,)), ((), ()))
TN = (((0,), (0,)), ((), ()))


def dot(a, b, dims=(((1,), (0,)), ((), ()))):
    return lax.dot_general(a, b, dims, preferred_element_type=F32)


def kernel(
    nz, ny, nx,
    a_ref, gain_ref, wq_ref, wk_ref, wv_ref, og_ref,
    out_ref, gg_ref,
    w0, w1, za, zg, sa, sg, xf, nrm, ogf, gmix,
    gains, gsum, gpart, gx, gy, gz, gsend, ig, part, xsend, xrecv, ysend, yrecv, zsend, zrecv,
    gain_low, l_s, w_s, w_r, p1_s, p1_r, p2_s, p2_r, az_s, az_r, ay_s, ay_r, ax_s, ax_r, ac_s, ac_r,
    oc_s, oc_r, gn_s, gn_r, pr_s, pr_r, xs_s, xs_r, gp_s, gp_r, gx_s, gx_r, gy_s, gy_r, gz_s, gz_r,
    oy_s, oy_r, oz_s, oz_r,
):
    frame = lax.axis_index("frames")
    x = lax.axis_index("heads")
    c = frame & 1
    y = (frame >> 1) & (ny - 1)
    z = frame >> (ny.bit_length())
    chip = z * ny + y
    width = a_ref.shape[1]
    model = width * nx
    tokens = 2 * nz * ny
    zrows = 2 * ny
    yrows = 2 * nz
    wrows = wq_ref.shape[0]
    crows = 2 * wrows
    ws = (w0, w1)

    def dev(z_, y_, c_, x_):
        return ((z_ * ny + y_) * 2 + c_, x_)

    def rcopy(src, dst, ssem, rsem, to):
        return pltpu.make_async_remote_copy(
            src_ref=src, dst_ref=dst, send_sem=ssem, recv_sem=rsem,
            device_id=to, device_id_type=pl.DeviceIdType.MESH,
        )

    def wrap(v, n):
        return v & (n - 1)

    def rows(v, m):
        return pl.ds(pl.multiple_of(v * m, m), m)

    def block(zb, yb):
        return rows(zb * ny + yb, crows)

    mate = dev(z, y, 1 - c, x)
    own_rows, mate_rows = rows(c, tokens), rows(1 - c, tokens)
    own_cols, all_cols = rows(x, width), pl.ds(0, width)

    def yp(o):
        return wrap(y + o, ny)

    def zp(o):
        return wrap(z + o, nz)

    def xp(o):
        return wrap(x + o, nx)

    def far(n):
        return sorted(range(1, n), key=lambda o: -min(o, n - o))

    arriving, leaving, local = {}, [], []

    def sent(copies):
        for copy in copies:
            copy.start()

    def expect(name, *waits):
        arriving[name] = waits

    def arrived(name):
        for wait in arriving.pop(name):
            wait()

    def landing(ref, rsem):
        return lambda: rcopy(ref, ref, rsem, rsem, mate).wait_recv()

    def left(ref, ssem):
        leaving.append(lambda: rcopy(ref, ref, ssem, ssem, mate).wait_send())

    def z_step(name, src, dst, s, r):
        sent(
            rcopy(src.at[rows(zp(o), zrows)], dst.at[rows(z, zrows)], s, r, dev(zp(o), y, c, x))
            for o in far(nz)
        )
        bulk = dst.at[pl.ds(0, (nz - 1) * zrows)]
        left(bulk, s)
        expect(name, landing(bulk, r))

    def y_step(name, src, dst, base, cols, s, r, by_piece=False):
        def place(at):
            return dst.at[pl.ds(pl.multiple_of(base + at * yrows, yrows), yrows), cols]

        sent(
            rcopy(
                src.at[rows(yp(o), yrows)], place(y), s, r.at[y] if by_piece else r, dev(z, yp(o), c, x)
            )
            for o in far(ny)
        )
        bulk = src.at[pl.ds(0, (ny - 1) * yrows)]
        left(bulk, s)
        if not by_piece:
            expect(name, landing(bulk, r))

    def swapped(value, na, nb):
        i = lax.broadcasted_iota(jnp.int32, (tokens, tokens), 0)
        j = lax.broadcasted_iota(jnp.int32, (tokens, tokens), 1)
        b = lax.div(i, 2 * na)
        a = lax.rem(lax.div(i, 2), na)
        hot = jnp.where(j == (a * nb + b) * 2 + lax.rem(i, 2), 1.0, 0.0).astype(BF16)
        return dot(hot, value).astype(BF16)

    def p1(j, o):
        ref = ws[j].at[block(z, y)]
        to = dev(z, yp(o), c, x) if j == 0 else dev(zp(o), y, c, x)
        return rcopy(ref, ref, p1_s.at[j, 0], p1_r.at[j, o], to)

    def p1_wait(j, o):
        landing(ws[j].at[block(z, yp(-o)) if j == 0 else block(zp(-o), y)], p1_r.at[j, o])()

    def place(j, d, age, k):
        sign = 1 if d == 0 else -1
        if j == 0:
            return ws[0].at[block(zp(-sign * age), wrap(y - k, ny))]
        return ws[1].at[block(wrap(z - k, nz), yp(-sign * age))]

    def p2(j, d, age, k):
        sign = 1 if d == 0 else -1
        to = dev(zp(sign), y, c, x) if j == 0 else dev(z, yp(sign), c, x)
        ref = place(j, d, age, k)
        return rcopy(ref, ref, p2_s.at[j, 0, 0, 0], p2_r.at[j, d, age, k], to)

    subs = ny
    last = nz // 2 - 1

    def goes(d, age, k):
        if age != last:
            return age < last
        return (k < subs // 2) if d == 0 else (k >= subs // 2)

    def each(act, halves=(0, 1)):
        for half in halves:
            @pl.loop(half * (subs // 2), (half + 1) * (subs // 2))
            def _(k):
                for j in range(2):
                    for d in range(2):
                        act(j, d, k, half * (subs - 1))

    def hop(age, halves=(0, 1)):
        def act(j, d, k, kind):
            if goes(d, age - 1, kind):
                landing(place(j, d, age, k), p2_r.at[j, d, age - 1, k])()
            if goes(d, age, kind):
                p2(j, d, age, k).start()

        each(act, halves)

    order = sorted(range(1, ny), key=lambda o: min(o, ny - o))

    def to_here(src, dst, n):
        copy = pltpu.make_async_copy(src, dst, l_s.at[n])
        copy.start()
        local.append(copy.wait)

    state = {}

    def drain():
        while leaving:
            leaving.pop(0)()

    def begin():
        for j in range(2):
            for i, w_ref in enumerate((wq_ref, wk_ref, wv_ref)):
                to_here(
                    w_ref.at[:, rows(2 * c + j, HDIM)],
                    ws[j].at[rows(2 * chip + c, wrows), i * HDIM:(i + 1) * HDIM],
                    3 * j + i,
                )
        to_here(a_ref.at[rows(z, zrows)], za.at[rows(z, zrows)], 6)
        to_here(og_ref.at[rows(z, zrows)], zg.at[rows(z, zrows)], 7)
        to_here(gain_ref, gain_low, 8)

        peers = [mate]
        peers += [dev(z, yp(o), c, x) for o in range(1, ny)]
        peers += [dev(zp(o), y, c, x) for o in range(1, nz)]
        peers += [dev(z, y, c, xp(o)) for o in range(1, nx)]
        bar = pltpu.get_barrier_semaphore()
        for to in peers:
            pl.semaphore_signal(bar, inc=1, device_id=to, device_id_type=pl.DeviceIdType.MESH)
        pl.semaphore_wait(bar, len(peers))

    def first_sends():
        for j in range(2):
            for i, w_ref in enumerate((wq_ref, wk_ref, wv_ref)):
                to = ws[j].at[rows(2 * chip + c, wrows), i * HDIM:(i + 1) * HDIM]
                sent([rcopy(w_ref.at[:, rows(2 * (1 - c) + j, HDIM)], to, w_s.at[j], w_r.at[j], mate)])
            ref = ws[j].at[rows(2 * chip + 1 - c, wrows)]
            left(ref, w_s.at[j])
            expect(("w", j), landing(ref, w_r.at[j]))
        z_step("az", a_ref, za, az_s, az_r)
        local.pop()()
        gains[x] = gain_low[...].astype(F32).reshape(1, width)
        sent(rcopy(gains.at[x], gains.at[x], gn_s, gn_r, dev(z, y, c, xp(o))) for o in far(nx))
        left(gains.at[pl.ds(0, nx - 1)], gn_s)
        expect("gains", landing(gains.at[pl.ds(0, nx - 1)], gn_r))

    def weights_own():
        for wait in local:
            wait()
        for j in range(2):
            arrived(("w", j))
            left(ws[j].at[pl.ds(0, (ny - 1) * crows)], p1_s.at[j, 0])
            count = sum(goes(d, age, k) for d in range(2) for age in range(last + 1) for k in range(subs))
            left(ws[j].at[pl.ds(0, count * crows)], p2_s.at[j, 0, 0, 0])
        for d in range(2):
            if goes(d, 0, 0):
                for j in range(2):
                    sent([p2(j, d, 0, 0)])
        for o in order:
            for j in range(2):
                sent([p1(j, o)])
        expect("p1", *(functools.partial(p1_wait, j, k) for k in order for j in range(2)))

    def act_y():
        arrived("az")
        sa[...] = swapped(za[...], nz, ny)
        y_step("ay", sa, xf, c * tokens, own_cols, ay_s.at[0], ay_r, True)
        xf[pl.ds(pl.multiple_of(c * tokens + y * yrows, yrows), yrows), own_cols] = sa[rows(y, yrows), :]

    def weights_0(ks):
        arriving.pop("p1", None)
        for k in ks:
            for j in range(2):
                p1_wait(j, k)
                for d in range(2):
                    if goes(d, 0, k):
                        sent([p2(j, d, 0, k)])

    def ac(at):
        ref = xf.at[own_rows, rows(at, width)]
        sent([rcopy(ref, ref, ac_s, ac_r, mate)])

    def act_x():
        def piece(at, cols):
            return xf.at[pl.ds(pl.multiple_of(c * tokens + at * yrows, yrows), yrows), cols]

        for oy in [0] + order:
            at = yp(oy)
            ref = piece(at, own_cols)
            if oy:
                landing(ref, ay_r.at[at])()
            sent(rcopy(ref, ref, ax_s.at[0], ax_r.at[x], dev(z, y, c, xp(o))) for o in far(nx))
        ac(x)
        for o in range(1, nx):
            ref = xf.at[own_rows, rows(xp(o), width)]
            expect(("ax", o), landing(ref, ax_r.at[xp(o)]))
            left(ref, ax_s.at[0])

    def grad_z():
        z_step("oz", og_ref, zg, oz_s.at[0], oz_r.at[0])

    def grad_y():
        arrived("oz")
        sg[0] = swapped(zg[...], nz, ny)
        y_step("oy", sg.at[0], sg.at[1], 0, all_cols, oy_s.at[0], oy_r.at[0])
        sg[1, rows(y, yrows), :] = sg[0, rows(y, yrows), :]

    def act_c():
        for o in reversed(far(nx)):
            arrived(("ax", o))
            ac(xp(o))

    def grad_c():
        arrived("oy")
        sent([rcopy(sg.at[1, :, rows(1 - c, 2 * HDIM)], ogf.at[own_rows], oc_s, oc_r, mate)])
        left(ogf.at[own_rows], oc_s)
        expect("oc", landing(ogf.at[mate_rows], oc_r))
        ogf[own_rows, :] = sg[1, :, rows(c, 2 * HDIM)]

    def norm():
        left(xf.at[own_rows], ac_s)
        landing(xf.at[mate_rows], ac_r)()
        arrived("gains")
        square_sum = jnp.zeros((2 * tokens, 1), F32)
        for at in range(nx):
            act = xf[:, at * width:(at + 1) * width].astype(F32)
            square_sum += jnp.sum(act * act, axis=1, keepdims=True)
        inverse_rms = lax.rsqrt(square_sum / model + EPS)
        for at in range(nx):
            act = xf[:, at * width:(at + 1) * width].astype(F32)
            nrm[:, at * width:(at + 1) * width] = (act * inverse_rms * gains[at]).astype(BF16)
        state["inverse_rms"] = inverse_rms

    def grad_wait():
        arrived("oc")

    def attention(h):
        i = lax.broadcasted_iota(jnp.int32, (2 * tokens, 1), 0)
        j = lax.broadcasted_iota(jnp.int32, (1, 2 * tokens), 1)

        def frame_of(r):
            core = lax.div(r, tokens)
            yy = lax.rem(lax.div(r, yrows), ny)
            zz = lax.rem(lax.div(r, 2), nz)
            return (zz * ny + yy) * 2 + core

        causal = (frame_of(i) >= frame_of(j)) & (lax.rem(i, 2) == lax.rem(j, 2))
        scale = HDIM ** (-0.5)
        proj = dot(nrm[...], ws[h][...])
        low = proj.astype(BF16)
        q, k, v = low[:, :HDIM], low[:, HDIM:2 * HDIM], low[:, 2 * HDIM:]
        g = ogf[:, h * HDIM:(h + 1) * HDIM]
        scores = dot(q, k, NT) * scale
        exps = jnp.where(causal, jnp.exp(jnp.where(causal, scores, 0.0)), 0.0)
        probs = exps / jnp.sum(exps, axis=1, keepdims=True)
        dprobs = dot(g, v, NT)
        delta = jnp.sum(probs * dprobs, axis=1, keepdims=True)
        dscores = (probs * (dprobs - delta) * scale).astype(BF16)
        gq = dot(dscores, k).astype(BF16)
        gk = dot(dscores, q, TN).astype(BF16)
        gv = dot(probs.astype(BF16), g, TN).astype(BF16)
        inner = state.get("inner", 0.0)
        for n, part_of in enumerate((gq, gk, gv)):
            gmix[h, :, n * HDIM:(n + 1) * HDIM] = part_of
            inner += jnp.sum(part_of.astype(F32) * proj[:, n * HDIM:(n + 1) * HDIM], axis=1, keepdims=True)
        state["inner"] = inner

    xorder = tuple(far(nx)) + (0,)

    def combine(b):
        arrived(("pr", b))
        o = xorder[b]
        total = ig[b, own_rows, :] + part[b]
        if b < nx - 1:
            xsend[b] = total.astype(BF16)
            sent([rcopy(xsend.at[b], xrecv.at[b], xs_s.at[b], xs_r.at[b], dev(z, y, c, xp(o)))])
            left(xsend.at[b], xs_s.at[b])
            expect(("xs", b), landing(xrecv.at[b], xs_r.at[b]))
        else:
            ig[b, own_rows, :] = total
        arrived(("gp", b))
        gsend[b] = gsum[b] + gpart[b]
        if b < nx - 1:
            sent([rcopy(gsend.at[b], gx.at[b], gx_s.at[b], gx_r.at[b], dev(z, y, c, xp(o)))])
            left(gsend.at[b], gx_s.at[b])
            expect(("gx", b), landing(gx.at[b], gx_r.at[b]))
        else:
            gx[b] = gsend[b]

    def backward():
        inner = state["inner"] / model
        inverse_rms = state["inverse_rms"]
        for b, o in enumerate(xorder):
            at = xp(o)
            feats = rows(at, width)
            gn = dot(gmix[0], w0[feats, :], NT) + dot(gmix[1], w1[feats, :], NT)
            act = xf[:, feats].astype(F32) * inverse_rms
            gsum[b] = jnp.sum(gn * act, axis=0, keepdims=True)
            ig[b] = inverse_rms * (gn * gains[at] - act * inner)
            sent([rcopy(ig.at[b, mate_rows], part.at[b], pr_s.at[b], pr_r.at[b], mate)])
            left(part.at[b], pr_s.at[b])
            expect(("pr", b), landing(part.at[b], pr_r.at[b]))
            sent([rcopy(gsum.at[b], gpart.at[b], gp_s.at[b], gp_r.at[b], mate)])
            left(gsum.at[b], gp_s.at[b])
            expect(("gp", b), landing(gpart.at[b], gp_r.at[b]))
            if b > 0:
                combine(b - 1)
        combine(nx - 1)

    def back_y():
        drain()
        total = ig[nx - 1, own_rows, :]
        for b in range(nx - 1):
            arrived(("xs", b))
            total += xrecv[b].astype(F32)
        ysend[...] = total.astype(BF16)
        y_step("by", ysend, yrecv, 0, all_cols, oy_s.at[1], oy_r.at[1])
        yrecv[rows(y, yrows), :] = ysend[rows(y, yrows), :]
        for b in range(nx - 1):
            arrived(("gx", b))
        gy[y] = jnp.sum(gx[...], axis=0)
        sent(rcopy(gy.at[y], gy.at[y], gy_s, gy_r, dev(z, yp(o), c, x)) for o in far(ny))
        left(gy.at[pl.ds(0, ny - 1)], gy_s)
        expect("gy", landing(gy.at[pl.ds(0, ny - 1)], gy_r))

    def back_z():
        arrived("by")
        zsend[...] = swapped(yrecv[...], ny, nz)
        z_step("bz", zsend, zrecv, oz_s.at[1], oz_r.at[1])
        zrecv[rows(z, zrows), :] = zsend[rows(z, zrows), :]
        arrived("gy")
        gz[z] = jnp.sum(gy[...], axis=0)
        sent(rcopy(gz.at[z], gz.at[z], gz_s, gz_r, dev(zp(o), y, c, x)) for o in far(nz))
        left(gz.at[pl.ds(0, nz - 1)], gz_s)
        expect("gz", landing(gz.at[pl.ds(0, nz - 1)], gz_r))

    def finish():
        drain()
        arrived("bz")
        out_ref[...] = zrecv[...]
        arrived("gz")
        gg_ref[...] = jnp.sum(gz[...], axis=0).reshape(width)

    step = functools.partial
    stages = [
        begin, first_sends, weights_own, step(weights_0, order[:4]), act_y, step(weights_0, order[4:]),
        grad_z, step(hop, 1), step(hop, 2, (0,)), act_x, step(hop, 2, (1,)), grad_y,
        step(hop, 3, (0,)), act_c, step(hop, 3, (1,)), norm, grad_c, step(hop, 4), grad_wait,
        step(attention, 0), step(attention, 1),
        backward, back_y, back_z, finish,
    ]
    for stage in stages:
        stage()
    drain()


def shards(nz, ny, nx, activations, norm_gain, w_query, w_key, w_value, out_grad):
    tokens, width = activations.shape
    model = width * nx
    wcols = 3 * HDIM
    wrows = w_query.shape[0]
    vmem = pl.BlockSpec(memory_space=pltpu.VMEM)
    hbm = pl.BlockSpec(memory_space=pltpu.HBM)
    dma = pltpu.SemaphoreType.DMA
    ring = nz // 2
    scratch = [
        pltpu.VMEM((model, wcols), BF16),
        pltpu.VMEM((model, wcols), BF16),
        pltpu.VMEM((tokens, width), BF16),
        pltpu.VMEM((tokens, width), BF16),
        pltpu.VMEM((tokens, width), BF16),
        pltpu.VMEM((2, tokens, width), BF16),
        pltpu.VMEM((2 * tokens, model), BF16),
        pltpu.VMEM((2 * tokens, model), BF16),
        pltpu.VMEM((2 * tokens, 2 * HDIM), BF16),
        pltpu.VMEM((2, 2 * tokens, wcols), BF16),
        pltpu.VMEM((nx, 1, width), F32),
        pltpu.VMEM((nx, 1, width), F32),
        pltpu.VMEM((nx, 1, width), F32),
        pltpu.VMEM((nx, 1, width), F32),
        pltpu.VMEM((ny, 1, width), F32),
        pltpu.VMEM((nz, 1, width), F32),
        pltpu.VMEM((nx, 1, width), F32),
        pltpu.VMEM((nx, 2 * tokens, width), F32),
        pltpu.VMEM((nx, tokens, width), F32),
        pltpu.VMEM((nx, tokens, width), BF16),
        pltpu.VMEM((nx, tokens, width), BF16),
        pltpu.VMEM((tokens, width), BF16),
        pltpu.VMEM((tokens, width), BF16),
        pltpu.VMEM((tokens, width), BF16),
        pltpu.VMEM((tokens, width), BF16),
    ]
    scratch += [pltpu.VMEM((width,), BF16), dma((9,))]
    for shape in (
        (2,), (2, ny), (2, 2, ring, ny), (), (ny,), (nx,), (),
        (), (), (nx,), (nx,), (nx,), (nx,), (), (),
        (2,), (2,),
    ):
        scratch += [dma(shape), dma(shape)] if shape else [dma, dma]
    args = (activations, norm_gain, w_query, w_key, w_value, out_grad)
    args = tuple(pltpu.with_memory_space_constraint(arg, pltpu.HBM) for arg in args)
    return pl.pallas_call(
        functools.partial(kernel, nz, ny, nx),
        out_shape=(
            jax.ShapeDtypeStruct((tokens, width), BF16),
            jax.ShapeDtypeStruct((width,), F32),
        ),
        in_specs=[hbm] * 6,
        out_specs=(vmem, vmem),
        scratch_shapes=scratch,
        compiler_params=pltpu.CompilerParams(
            collective_id=0, has_side_effects=True, vmem_limit_bytes=24 * 1024 * 1024
        ),
    )(*args)


def solution(mesh, nz=8, ny=8):
    nx = mesh.shape["heads"]
    in_specs = (
        P("frames", "heads"),
        P("heads"),
        P("frames", "heads"),
        P("frames", "heads"),
        P("frames", "heads"),
        P("frames", "heads"),
    )
    out_specs = (P("frames", "heads"), P("heads"))
    return jax.shard_map(
        functools.partial(shards, nz, ny, nx),
        mesh=mesh, in_specs=in_specs, out_specs=out_specs, check_vma=False,
    )
```

```python
import functools

import jax
import jax.numpy as jnp
from jax import lax
from jax.experimental import pallas as pl
from jax.experimental.pallas import tpu as pltpu
from jax.sharding import PartitionSpec as P

EPS = 1e-05
HDIM = 128
F32 = jnp.float32
BF16 = jnp.bfloat16
NT = (((1,), (1,)), ((), ()))
TN = (((0,), (0,)), ((), ()))


def dot(a, b, dims=(((1,), (0,)), ((), ()))):
    return lax.dot_general(a, b, dims, preferred_element_type=F32)


def kernel(
    nz, ny, nx,
    a_ref, gain_ref, wq_ref, wk_ref, wv_ref, og_ref,
    out_ref, gg_ref,
    w0, w1, za, zg, sa, sg, xf, nrm, ogf, gmix,
    gains, gsum, gpart, gx, gy, gz, gsend, ig, part, xsend, xrecv, ysend, yrecv, zsend, zrecv,
    gain_low, hot, l_s, w_s, w_r, p1_s, p1_r, p2_s, p2_r, az_s, az_r, ay_s, ay_r, ax_s, ax_r, ac_s, ac_r,
    oc_s, oc_r, gn_s, gn_r, pr_s, pr_r, xs_s, xs_r, gp_s, gp_r, gx_s, gx_r, gy_s, gy_r, gz_s, gz_r,
    oy_s, oy_r, oz_s, oz_r,
):
    frame = lax.axis_index("frames")
    x = lax.axis_index("heads")
    c = frame & 1
    y = (frame >> 1) & (ny - 1)
    z = frame >> (ny.bit_length())
    chip = z * ny + y
    width = a_ref.shape[1]
    model = width * nx
    tokens = 2 * nz * ny
    zrows = 2 * ny
    yrows = 2 * nz
    wrows = wq_ref.shape[0]
    crows = 2 * wrows
    ws = (w0, w1)

    def dev(z_, y_, c_, x_):
        return ((z_ * ny + y_) * 2 + c_, x_)

    def rcopy(src, dst, ssem, rsem, to):
        return pltpu.make_async_remote_copy(
            src_ref=src, dst_ref=dst, send_sem=ssem, recv_sem=rsem,
            device_id=to, device_id_type=pl.DeviceIdType.MESH,
        )

    def wrap(v, n):
        return v & (n - 1)

    def rows(v, m):
        return pl.ds(pl.multiple_of(v * m, m), m)

    def block(zb, yb):
        return rows(zb * ny + yb, crows)

    mate = dev(z, y, 1 - c, x)
    own_rows, mate_rows = rows(c, tokens), rows(1 - c, tokens)
    own_cols, all_cols = rows(x, width), pl.ds(0, width)

    def yp(o):
        return wrap(y + o, ny)

    def zp(o):
        return wrap(z + o, nz)

    def xp(o):
        return wrap(x + o, nx)

    def far(n):
        return sorted(range(1, n), key=lambda o: -min(o, n - o))

    arriving, leaving, local = {}, [], []

    def sent(copies):
        for copy in copies:
            copy.start()

    def expect(name, *waits):
        arriving[name] = waits

    def arrived(name):
        for wait in arriving.pop(name):
            wait()

    def landing(ref, rsem):
        return lambda: rcopy(ref, ref, rsem, rsem, mate).wait_recv()

    def left(ref, ssem):
        leaving.append(lambda: rcopy(ref, ref, ssem, ssem, mate).wait_send())

    def z_step(name, src, dst, s, r):
        sent(
            rcopy(src.at[rows(zp(o), zrows)], dst.at[rows(z, zrows)], s, r, dev(zp(o), y, c, x))
            for o in far(nz)
        )
        bulk = dst.at[pl.ds(0, (nz - 1) * zrows)]
        left(bulk, s)
        expect(name, landing(bulk, r))

    def y_step(name, src, dst, base, cols, s, r, by_piece=False):
        def place(at):
            return dst.at[pl.ds(pl.multiple_of(base + at * yrows, yrows), yrows), cols]

        sent(
            rcopy(
                src.at[rows(yp(o), yrows)], place(y), s, r.at[y] if by_piece else r, dev(z, yp(o), c, x)
            )
            for o in far(ny)
        )
        bulk = src.at[pl.ds(0, (ny - 1) * yrows)]
        left(bulk, s)
        if not by_piece:
            expect(name, landing(bulk, r))

    def swap_rows(back):
        i = lax.broadcasted_iota(jnp.int32, (tokens, tokens), 1 if back else 0)
        j = lax.broadcasted_iota(jnp.int32, (tokens, tokens), 0 if back else 1)
        bits = nz.bit_length()
        source = (i & (nz - 1)) * zrows + (i >> bits) * 2 + ((i >> (bits - 1)) & 1)
        return jnp.where(j == source, 1.0, 0.0).astype(BF16)

    def swapped(value, back=0):
        return dot(hot[back], value).astype(BF16)

    def of_position(value, p):
        split = value.reshape(2 * ny, 2, nz, value.shape[1])
        return split[:, p].reshape(tokens, value.shape[1])

    def p1(j, o):
        ref = ws[j].at[block(z, y)]
        to = dev(z, yp(o), c, x) if j == 0 else dev(zp(o), y, c, x)
        return rcopy(ref, ref, p1_s.at[j, 0], p1_r.at[j, o], to)

    def p1_wait(j, o):
        landing(ws[j].at[block(z, yp(-o)) if j == 0 else block(zp(-o), y)], p1_r.at[j, o])()

    def place(j, d, age, k):
        sign = 1 if d == 0 else -1
        if j == 0:
            return ws[0].at[block(zp(-sign * age), wrap(y - k, ny))]
        return ws[1].at[block(wrap(z - k, nz), yp(-sign * age))]

    def p2(j, d, age, k):
        sign = 1 if d == 0 else -1
        to = dev(zp(sign), y, c, x) if j == 0 else dev(z, yp(sign), c, x)
        ref = place(j, d, age, k)
        return rcopy(ref, ref, p2_s.at[j, 0, 0, 0], p2_r.at[j, d, age, k], to)

    subs = ny
    last = nz // 2 - 1

    def goes(d, age, k):
        if age != last:
            return age < last
        return (k < subs // 2) if d == 0 else (k >= subs // 2)

    def each(act, halves=(0, 1)):
        for half in halves:
            @pl.loop(half * (subs // 2), (half + 1) * (subs // 2))
            def _(k):
                for j in range(2):
                    for d in range(2):
                        act(j, d, k, half * (subs - 1))

    def hop(age, halves=(0, 1)):
        def act(j, d, k, kind):
            if goes(d, age - 1, kind):
                landing(place(j, d, age, k), p2_r.at[j, d, age - 1, k])()
            if goes(d, age, kind):
                p2(j, d, age, k).start()

        each(act, halves)

    def last_hop(j):
        for k in range(subs):
            for d in range(2):
                if goes(d, last, k):
                    landing(place(j, d, last + 1, k), p2_r.at[j, d, last, k])()

    order = sorted(range(1, ny), key=lambda o: min(o, ny - o))

    def to_here(src, dst, n):
        copy = pltpu.make_async_copy(src, dst, l_s.at[n])
        copy.start()
        local.append(copy.wait)

    state = {}

    def drain():
        while leaving:
            leaving.pop(0)()

    def begin():
        for j in range(2):
            for i, w_ref in enumerate((wq_ref, wk_ref, wv_ref)):
                to_here(
                    w_ref.at[:, rows(2 * c + j, HDIM)],
                    ws[j].at[rows(2 * chip + c, wrows), i * HDIM:(i + 1) * HDIM],
                    3 * j + i,
                )
        to_here(a_ref.at[rows(z, zrows)], za.at[rows(z, zrows)], 6)
        to_here(og_ref.at[rows(z, zrows)], zg.at[rows(z, zrows)], 7)
        to_here(gain_ref, gain_low, 8)

        hot[0] = swap_rows(False)
        hot[1] = swap_rows(True)

        peers = [mate]
        peers += [dev(z, yp(o), c, x) for o in range(1, ny)]
        peers += [dev(zp(o), y, c, x) for o in range(1, nz)]
        peers += [dev(z, y, c, xp(o)) for o in range(1, nx)]
        bar = pltpu.get_barrier_semaphore()
        for to in peers:
            pl.semaphore_signal(bar, inc=1, device_id=to, device_id_type=pl.DeviceIdType.MESH)
        pl.semaphore_wait(bar, len(peers))

    def first_sends():
        for j in range(2):
            for i, w_ref in enumerate((wq_ref, wk_ref, wv_ref)):
                to = ws[j].at[rows(2 * chip + c, wrows), i * HDIM:(i + 1) * HDIM]
                sent([rcopy(w_ref.at[:, rows(2 * (1 - c) + j, HDIM)], to, w_s.at[j], w_r.at[j], mate)])
            ref = ws[j].at[rows(2 * chip + 1 - c, wrows)]
            left(ref, w_s.at[j])
            expect(("w", j), landing(ref, w_r.at[j]))
        z_step("az", a_ref, za, az_s, az_r)
        local.pop()()
        gains[x] = gain_low[...].astype(F32).reshape(1, width)
        sent(rcopy(gains.at[x], gains.at[x], gn_s, gn_r, dev(z, y, c, xp(o))) for o in far(nx))
        left(gains.at[pl.ds(0, nx - 1)], gn_s)
        expect("gains", landing(gains.at[pl.ds(0, nx - 1)], gn_r))

    def weights_own():
        for wait in local:
            wait()
        for j in range(2):
            arrived(("w", j))
            left(ws[j].at[pl.ds(0, (ny - 1) * crows)], p1_s.at[j, 0])
            count = sum(goes(d, age, k) for d in range(2) for age in range(last + 1) for k in range(subs))
            left(ws[j].at[pl.ds(0, count * crows)], p2_s.at[j, 0, 0, 0])
        for d in range(2):
            if goes(d, 0, 0):
                for j in range(2):
                    sent([p2(j, d, 0, 0)])
        for o in order:
            for j in range(2):
                sent([p1(j, o)])
        expect("p1", *(functools.partial(p1_wait, j, k) for k in order for j in range(2)))

    def act_y():
        arrived("az")
        sa[...] = swapped(za[...])
        y_step("ay", sa, xf, c * tokens, own_cols, ay_s.at[0], ay_r, True)
        xf[pl.ds(pl.multiple_of(c * tokens + y * yrows, yrows), yrows), own_cols] = sa[rows(y, yrows), :]

    def weights_0(ks):
        arriving.pop("p1", None)
        for k in ks:
            for j in range(2):
                p1_wait(j, k)
                for d in range(2):
                    if goes(d, 0, k):
                        sent([p2(j, d, 0, k)])

    def ac(at):
        ref = xf.at[own_rows, rows(at, width)]
        sent([rcopy(ref, ref, ac_s, ac_r, mate)])

    def act_x():
        def piece(at, cols):
            return xf.at[pl.ds(pl.multiple_of(c * tokens + at * yrows, yrows), yrows), cols]

        for oy in [0] + order:
            at = yp(oy)
            ref = piece(at, own_cols)
            if oy:
                landing(ref, ay_r.at[at])()
            sent(rcopy(ref, ref, ax_s.at[0], ax_r.at[x], dev(z, y, c, xp(o))) for o in far(nx))
        ac(x)
        for o in range(1, nx):
            ref = xf.at[own_rows, rows(xp(o), width)]
            expect(("ax", o), landing(ref, ax_r.at[xp(o)]))
            left(ref, ax_s.at[0])

    def grad_z():
        z_step("oz", og_ref, zg, oz_s.at[0], oz_r.at[0])

    def grad_y():
        arrived("oz")
        sg[0] = swapped(zg[...])
        y_step("oy", sg.at[0], sg.at[1], 0, all_cols, oy_s.at[0], oy_r.at[0])
        sg[1, rows(y, yrows), :] = sg[0, rows(y, yrows), :]

    def act_c():
        for o in reversed(far(nx)):
            arrived(("ax", o))
            ac(xp(o))

    def grad_c():
        arrived("oy")
        sent([rcopy(sg.at[1, :, rows(1 - c, 2 * HDIM)], ogf.at[own_rows], oc_s, oc_r, mate)])
        left(ogf.at[own_rows], oc_s)
        expect("oc", landing(ogf.at[mate_rows], oc_r))
        ogf[own_rows, :] = sg[1, :, rows(c, 2 * HDIM)]

    def norm():
        left(xf.at[own_rows], ac_s)
        landing(xf.at[mate_rows], ac_r)()
        arrived("gains")
        square_sum = jnp.zeros((2 * tokens, 1), F32)
        for at in range(nx):
            act = xf[:, at * width:(at + 1) * width].astype(F32)
            square_sum += jnp.sum(act * act, axis=1, keepdims=True)
        inverse_rms = lax.rsqrt(square_sum / model + EPS)
        for at in range(nx):
            act = xf[:, at * width:(at + 1) * width].astype(F32)
            nrm[:, at * width:(at + 1) * width] = (act * inverse_rms * gains[at]).astype(BF16)
        state["inverse_rms"] = inverse_rms

    def grad_wait():
        arrived("oc")

    def project(h):
        proj = dot(nrm[...], ws[h][...])
        for p in range(2):
            state["proj", p, h] = of_position(proj, p)

    def attention(p):
        i = lax.broadcasted_iota(jnp.int32, (tokens, 1), 0)
        j = lax.broadcasted_iota(jnp.int32, (1, tokens), 1)

        def frame_of(r):
            return ((r & (nz - 1)) * ny + (lax.div(r, nz) & (ny - 1))) * 2 + lax.div(r, nz * ny)

        causal = frame_of(i) >= frame_of(j)
        scale = HDIM ** (-0.5)
        inner = jnp.zeros((tokens, 1), F32)
        for h in range(2):
            proj = state["proj", p, h]
            low = proj.astype(BF16)
            q, k, v = low[:, :HDIM], low[:, HDIM:2 * HDIM], low[:, 2 * HDIM:]
            g = of_position(ogf[:, h * HDIM:(h + 1) * HDIM].astype(F32), p).astype(BF16)
            scores = dot(q, k, NT) * scale
            exps = jnp.where(causal, jnp.exp(jnp.where(causal, scores, 0.0)), 0.0)
            probs = exps / jnp.sum(exps, axis=1, keepdims=True)
            dprobs = dot(g, v, NT)
            delta = jnp.sum(probs * dprobs, axis=1, keepdims=True)
            dscores = (probs * (dprobs - delta) * scale).astype(BF16)
            gq = dot(dscores, k).astype(BF16)
            gk = dot(dscores, q, TN).astype(BF16)
            gv = dot(probs.astype(BF16), g, TN).astype(BF16)
            for n, part_of in enumerate((gq, gk, gv)):
                gmix[p, h, :, n * HDIM:(n + 1) * HDIM] = part_of
                inner += jnp.sum(part_of.astype(F32) * proj[:, n * HDIM:(n + 1) * HDIM], axis=1, keepdims=True)
        state["inner", p] = inner / model

    xorder = tuple(far(nx)) + (0,)
    half = tokens // 2

    def combine(p, b):
        arrived(("pr", p, b))
        o = xorder[b]
        total = ig[p, b, rows(c, half), :] + part[p, b]
        if b < nx - 1:
            xsend[p, b] = total.astype(BF16)
            sems = xs_s.at[p, b], xs_r.at[p, b]
            sent([rcopy(xsend.at[p, b], xrecv.at[p, b], *sems, dev(z, y, c, xp(o)))])
            left(xsend.at[p, b], sems[0])
            expect(("xs", p, b), landing(xrecv.at[p, b], sems[1]))
        else:
            ig[p, b, rows(c, half), :] = total

    def backward(p):
        inner = state["inner", p]
        inverse_rms = of_position(state["inverse_rms"], p)
        for b, o in enumerate(xorder):
            at = xp(o)
            feats = rows(at, width)
            gn = dot(gmix[p, 0], w0[feats, :], NT) + dot(gmix[p, 1], w1[feats, :], NT)
            act = of_position(xf[:, feats].astype(F32), p) * inverse_rms
            terms = jnp.sum(gn * act, axis=0, keepdims=True)
            gsum[b] = gsum[b] + terms if p else terms
            ig[p, b] = inverse_rms * (gn * gains[at] - act * inner)
            sems = pr_s.at[p, b], pr_r.at[p, b]
            sent([rcopy(ig.at[p, b, rows(1 - c, half)], part.at[p, b], *sems, mate)])
            left(part.at[p, b], sems[0])
            expect(("pr", p, b), landing(part.at[p, b], sems[1]))
            if p and b > 0:
                combine(p, b - 1)

    def combine_first():
        for b in range(nx):
            combine(0, b)

    def combine_last():
        sent([rcopy(gsum, gpart, gp_s.at[0], gp_r.at[0], mate)])
        early, leaving[:] = leaving[:], []
        left(gsum, gp_s.at[0])
        combine(1, nx - 1)
        landing(gpart, gp_r.at[0])()
        gsend[...] = gsum[...] + gpart[...]
        gx[nx - 1] = gsend[nx - 1]
        sent(
            rcopy(gsend.at[b], gx.at[b], gx_s.at[0], gx_r.at[0], dev(z, y, c, xp(xorder[b]))) for b in range(nx - 1)
        )
        left(gsend.at[pl.ds(0, nx - 1)], gx_s.at[0])
        expect("gx", landing(gx.at[pl.ds(0, nx - 1)], gx_r.at[0]))
        for wait in early:
            wait()

    def back_y():
        totals = []
        for p in range(2):
            total = ig[p, nx - 1, rows(c, half), :]
            for b in range(nx - 1):
                arrived(("xs", p, b))
                total += xrecv[p, b].astype(F32)
            totals.append(total.reshape(ny, 1, nz, width))
        ysend[...] = jnp.concatenate(totals, axis=1).reshape(tokens, width).astype(BF16)
        y_step("by", ysend, yrecv, 0, all_cols, oy_s.at[1], oy_r.at[1])
        yrecv[rows(y, yrows), :] = ysend[rows(y, yrows), :]
        arrived("gx")
        gy[y] = jnp.sum(gx[...], axis=0)
        sent(rcopy(gy.at[y], gy.at[y], gy_s, gy_r, dev(z, yp(o), c, x)) for o in far(ny))
        left(gy.at[pl.ds(0, ny - 1)], gy_s)
        expect("gy", landing(gy.at[pl.ds(0, ny - 1)], gy_r))
        drain()

    def back_z():
        arrived("by")
        zsend[...] = swapped(yrecv[...], 1)
        z_step("bz", zsend, zrecv, oz_s.at[1], oz_r.at[1])
        zrecv[rows(z, zrows), :] = zsend[rows(z, zrows), :]
        arrived("gy")
        gz[z] = jnp.sum(gy[...], axis=0)
        sent(rcopy(gz.at[z], gz.at[z], gz_s, gz_r, dev(zp(o), y, c, x)) for o in far(nz))
        left(gz.at[pl.ds(0, nz - 1)], gz_s)
        expect("gz", landing(gz.at[pl.ds(0, nz - 1)], gz_r))

    def finish():
        arrived("bz")
        out_ref[...] = zrecv[...]
        arrived("gz")
        gg_ref[...] = jnp.sum(gz[...], axis=0).reshape(width)

    step = functools.partial
    stages = [
        begin, first_sends, weights_own, step(weights_0, order), act_y, step(hop, 1), act_x, grad_z,
        step(hop, 2), act_c, grad_y, step(hop, 3), grad_c, norm,
        step(last_hop, 0), step(project, 0), step(last_hop, 1), step(project, 1), grad_wait,
        step(attention, 0), step(backward, 0), combine_first, step(attention, 1), step(backward, 1), combine_last,
        back_y, back_z, finish,
    ]
    for stage in stages:
        stage()
    drain()


def shards(nz, ny, nx, activations, norm_gain, w_query, w_key, w_value, out_grad):
    tokens, width = activations.shape
    model = width * nx
    wcols = 3 * HDIM
    wrows = w_query.shape[0]
    vmem = pl.BlockSpec(memory_space=pltpu.VMEM)
    hbm = pl.BlockSpec(memory_space=pltpu.HBM)
    dma = pltpu.SemaphoreType.DMA
    ring = nz // 2
    scratch = [
        pltpu.VMEM((model, wcols), BF16),
        pltpu.VMEM((model, wcols), BF16),
        pltpu.VMEM((tokens, width), BF16),
        pltpu.VMEM((tokens, width), BF16),
        pltpu.VMEM((tokens, width), BF16),
        pltpu.VMEM((2, tokens, width), BF16),
        pltpu.VMEM((2 * tokens, model), BF16),
        pltpu.VMEM((2 * tokens, model), BF16),
        pltpu.VMEM((2 * tokens, 2 * HDIM), BF16),
        pltpu.VMEM((2, 2, tokens, wcols), BF16),
        pltpu.VMEM((nx, 1, width), F32),
        pltpu.VMEM((nx, 1, width), F32),
        pltpu.VMEM((nx, 1, width), F32),
        pltpu.VMEM((nx, 1, width), F32),
        pltpu.VMEM((ny, 1, width), F32),
        pltpu.VMEM((nz, 1, width), F32),
        pltpu.VMEM((nx, 1, width), F32),
        pltpu.VMEM((2, nx, tokens, width), F32),
        pltpu.VMEM((2, nx, tokens // 2, width), F32),
        pltpu.VMEM((2, nx, tokens // 2, width), BF16),
        pltpu.VMEM((2, nx, tokens // 2, width), BF16),
        pltpu.VMEM((tokens, width), BF16),
        pltpu.VMEM((tokens, width), BF16),
        pltpu.VMEM((tokens, width), BF16),
        pltpu.VMEM((tokens, width), BF16),
    ]
    scratch += [pltpu.VMEM((width,), BF16), pltpu.VMEM((2, tokens, tokens), BF16), dma((9,))]
    for shape in (
        (2,), (2, ny), (2, 2, ring, ny), (), (ny,), (nx,), (),
        (), (), (2, nx), (2, nx), (nx,), (nx,), (), (),
        (2,), (2,),
    ):
        scratch += [dma(shape), dma(shape)] if shape else [dma, dma]
    args = (activations, norm_gain, w_query, w_key, w_value, out_grad)
    args = tuple(pltpu.with_memory_space_constraint(arg, pltpu.HBM) for arg in args)
    return pl.pallas_call(
        functools.partial(kernel, nz, ny, nx),
        out_shape=(
            jax.ShapeDtypeStruct((tokens, width), BF16),
            jax.ShapeDtypeStruct((width,), F32),
        ),
        in_specs=[hbm] * 6,
        out_specs=(vmem, vmem),
        scratch_shapes=scratch,
        compiler_params=pltpu.CompilerParams(
            collective_id=0, has_side_effects=True, vmem_limit_bytes=24 * 1024 * 1024
        ),
    )(*args)


def solution(mesh, nz=8, ny=8):
    nx = mesh.shape["heads"]
    in_specs = (
        P("frames", "heads"),
        P("heads"),
        P("frames", "heads"),
        P("frames", "heads"),
        P("frames", "heads"),
        P("frames", "heads"),
    )
    out_specs = (P("frames", "heads"), P("heads"))
    return jax.shard_map(
        functools.partial(shards, nz, ny, nx),
        mesh=mesh, in_specs=in_specs, out_specs=out_specs, check_vma=False,
    )
```

```python
import functools

import jax
import jax.numpy as jnp
from jax import lax
from jax.experimental import pallas as pl
from jax.experimental.pallas import tpu as pltpu
from jax.sharding import PartitionSpec as P

EPS = 1e-05
HDIM = 128
F32 = jnp.float32
BF16 = jnp.bfloat16
NT = (((1,), (1,)), ((), ()))
TN = (((0,), (0,)), ((), ()))


def dot(a, b, dims=(((1,), (0,)), ((), ()))):
    return lax.dot_general(a, b, dims, preferred_element_type=F32)


def kernel(
    nz, ny, nx,
    a_ref, gain_ref, wq_ref, wk_ref, wv_ref, og_ref,
    out_ref, gg_ref,
    w0, w1, za, zg, sa, sg, xf, nrm, ogf, gmix,
    gains, gsum, gpart, gx, gy, gz, gsend, ig, part, xsend, xrecv, ysend, yrecv, zsend, zrecv,
    gain_low, hot, l_s, w_s, w_r, p1_s, p1_r, p2_s, p2_r, az_s, az_r, ay_s, ay_r, ax_s, ax_r, ac_s, ac_r,
    oc_s, oc_r, gn_s, gn_r, pr_s, pr_r, xs_s, xs_r, gp_s, gp_r, gx_s, gx_r, gy_s, gy_r, gz_s, gz_r,
    oy_s, oy_r, oz_s, oz_r,
):
    frame = lax.axis_index("frames")
    x = lax.axis_index("heads")
    c = frame & 1
    y = (frame >> 1) & (ny - 1)
    z = frame >> (ny.bit_length())
    chip = z * ny + y
    width = a_ref.shape[1]
    model = width * nx
    tokens = 2 * nz * ny
    zrows = 2 * ny
    yrows = 2 * nz
    wrows = wq_ref.shape[0]
    crows = 2 * wrows
    ws = (w0, w1)

    def dev(z_, y_, c_, x_):
        return ((z_ * ny + y_) * 2 + c_, x_)

    def rcopy(src, dst, ssem, rsem, to):
        return pltpu.make_async_remote_copy(
            src_ref=src, dst_ref=dst, send_sem=ssem, recv_sem=rsem,
            device_id=to, device_id_type=pl.DeviceIdType.MESH,
        )

    def wrap(v, n):
        return v & (n - 1)

    def rows(v, m):
        return pl.ds(pl.multiple_of(v * m, m), m)

    def block(zb, yb):
        return rows(zb * ny + yb, crows)

    mate = dev(z, y, 1 - c, x)
    own_rows, mate_rows = rows(c, tokens), rows(1 - c, tokens)
    own_cols, all_cols = rows(x, width), pl.ds(0, width)

    def yp(o):
        return wrap(y + o, ny)

    def zp(o):
        return wrap(z + o, nz)

    def xp(o):
        return wrap(x + o, nx)

    def far(n):
        return sorted(range(1, n), key=lambda o: -min(o, n - o))

    arriving, leaving, local = {}, [], []

    def sent(copies):
        for copy in copies:
            copy.start()

    def expect(name, *waits):
        arriving[name] = waits

    def arrived(name):
        for wait in arriving.pop(name):
            wait()

    def landing(ref, rsem):
        return lambda: rcopy(ref, ref, rsem, rsem, mate).wait_recv()

    def left(ref, ssem):
        leaving.append(lambda: rcopy(ref, ref, ssem, ssem, mate).wait_send())

    def z_step(name, src, dst, s, r):
        sent(
            rcopy(src.at[rows(zp(o), zrows)], dst.at[rows(z, zrows)], s, r, dev(zp(o), y, c, x))
            for o in far(nz)
        )
        bulk = dst.at[pl.ds(0, (nz - 1) * zrows)]
        left(bulk, s)
        expect(name, landing(bulk, r))

    def y_step(name, src, dst, base, cols, s, r, by_piece=False):
        def place(at):
            return dst.at[pl.ds(pl.multiple_of(base + at * yrows, yrows), yrows), cols]

        sent(
            rcopy(
                src.at[rows(yp(o), yrows)], place(y), s, r.at[y] if by_piece else r, dev(z, yp(o), c, x)
            )
            for o in far(ny)
        )
        bulk = src.at[pl.ds(0, (ny - 1) * yrows)]
        left(bulk, s)
        if not by_piece:
            expect(name, landing(bulk, r))

    def swap_rows(back):
        i = lax.broadcasted_iota(jnp.int32, (tokens, tokens), 1 if back else 0)
        j = lax.broadcasted_iota(jnp.int32, (tokens, tokens), 0 if back else 1)
        bits = nz.bit_length()
        source = (i & (nz - 1)) * zrows + (i >> bits) * 2 + ((i >> (bits - 1)) & 1)
        return jnp.where(j == source, 1.0, 0.0).astype(BF16)

    def swapped(value, back=0):
        return dot(hot[back], value).astype(BF16)

    def of_position(value, p):
        split = value.reshape(2 * ny, 2, nz, value.shape[1])
        return split[:, p].reshape(tokens, value.shape[1])

    def p1(j, o):
        ref = ws[j].at[block(z, y)]
        to = dev(z, yp(o), c, x) if j == 0 else dev(zp(o), y, c, x)
        return rcopy(ref, ref, p1_s.at[j, 0], p1_r.at[j, o], to)

    def p1_wait(j, o):
        landing(ws[j].at[block(z, yp(-o)) if j == 0 else block(zp(-o), y)], p1_r.at[j, o])()

    def place(j, d, age, k):
        sign = 1 if d == 0 else -1
        if j == 0:
            return ws[0].at[block(zp(-sign * age), wrap(y - k, ny))]
        return ws[1].at[block(wrap(z - k, nz), yp(-sign * age))]

    def p2(j, d, age, k):
        sign = 1 if d == 0 else -1
        to = dev(zp(sign), y, c, x) if j == 0 else dev(z, yp(sign), c, x)
        ref = place(j, d, age, k)
        return rcopy(ref, ref, p2_s.at[j, 0, 0, 0], p2_r.at[j, d, age, k], to)

    subs = ny
    last = nz // 2 - 1

    def goes(d, age, k):
        if age != last:
            return age < last
        return (k < subs // 2) if d == 0 else (k >= subs // 2)

    def each(act, halves=(0, 1)):
        for half in halves:
            @pl.loop(half * (subs // 2), (half + 1) * (subs // 2))
            def _(k):
                for j in range(2):
                    for d in range(2):
                        act(j, d, k, half * (subs - 1))

    def hop(age, halves=(0, 1)):
        def act(j, d, k, kind):
            if goes(d, age - 1, kind):
                landing(place(j, d, age, k), p2_r.at[j, d, age - 1, k])()
            if goes(d, age, kind):
                p2(j, d, age, k).start()

        each(act, halves)

    def last_hop(j):
        for k in range(subs):
            for d in range(2):
                if goes(d, last, k):
                    landing(place(j, d, last + 1, k), p2_r.at[j, d, last, k])()

    order = sorted(range(1, ny), key=lambda o: min(o, ny - o))

    def to_here(src, dst, n):
        copy = pltpu.make_async_copy(src, dst, l_s.at[n])
        copy.start()
        local.append(copy.wait)

    state = {}

    def drain():
        while leaving:
            leaving.pop(0)()

    def begin():
        peers = [mate]
        peers += [dev(z, yp(o), c, x) for o in range(1, ny)]
        peers += [dev(zp(o), y, c, x) for o in range(1, nz)]
        peers += [dev(z, y, c, xp(o)) for o in range(1, nx)]
        bar = pltpu.get_barrier_semaphore()
        for to in peers:
            pl.semaphore_signal(bar, inc=1, device_id=to, device_id_type=pl.DeviceIdType.MESH)

        for j in range(2):
            for i, w_ref in enumerate((wq_ref, wk_ref, wv_ref)):
                to_here(
                    w_ref.at[:, rows(2 * c + j, HDIM)],
                    ws[j].at[rows(2 * chip + c, wrows), i * HDIM:(i + 1) * HDIM],
                    3 * j + i,
                )
        to_here(a_ref.at[rows(z, zrows)], za.at[rows(z, zrows)], 6)
        to_here(og_ref.at[rows(z, zrows)], zg.at[rows(z, zrows)], 7)
        to_here(gain_ref, gain_low, 8)

        hot[0] = swap_rows(False)
        hot[1] = swap_rows(True)
        pl.semaphore_wait(bar, len(peers))

    def first_sends():
        for j in range(2):
            for i, w_ref in enumerate((wq_ref, wk_ref, wv_ref)):
                to = ws[j].at[rows(2 * chip + c, wrows), i * HDIM:(i + 1) * HDIM]
                sent([rcopy(w_ref.at[:, rows(2 * (1 - c) + j, HDIM)], to, w_s.at[j], w_r.at[j], mate)])
            ref = ws[j].at[rows(2 * chip + 1 - c, wrows)]
            left(ref, w_s.at[j])
            expect(("w", j), landing(ref, w_r.at[j]))
        z_step("az", a_ref, za, az_s, az_r)
        local.pop()()
        gains[x] = gain_low[...].astype(F32).reshape(1, width)
        sent(rcopy(gains.at[x], gains.at[x], gn_s, gn_r, dev(z, y, c, xp(o))) for o in far(nx))
        left(gains.at[pl.ds(0, nx - 1)], gn_s)
        expect("gains", landing(gains.at[pl.ds(0, nx - 1)], gn_r))

    def weights_own():
        for wait in local:
            wait()
        for j in range(2):
            arrived(("w", j))
            left(ws[j].at[pl.ds(0, (ny - 1) * crows)], p1_s.at[j, 0])
            count = sum(goes(d, age, k) for d in range(2) for age in range(last + 1) for k in range(subs))
            left(ws[j].at[pl.ds(0, count * crows)], p2_s.at[j, 0, 0, 0])
        for d in range(2):
            if goes(d, 0, 0):
                for j in range(2):
                    sent([p2(j, d, 0, 0)])
        for o in order:
            for j in range(2):
                sent([p1(j, o)])
        expect("p1", *(functools.partial(p1_wait, j, k) for k in order for j in range(2)))

    def act_y():
        arrived("az")
        sa[...] = swapped(za[...])
        y_step("ay", sa, xf, c * tokens, own_cols, ay_s.at[0], ay_r, True)
        xf[pl.ds(pl.multiple_of(c * tokens + y * yrows, yrows), yrows), own_cols] = sa[rows(y, yrows), :]

    def weights_0(ks):
        arriving.pop("p1", None)
        for k in ks:
            for j in range(2):
                p1_wait(j, k)
                for d in range(2):
                    if goes(d, 0, k):
                        sent([p2(j, d, 0, k)])

    def ac(at):
        ref = xf.at[own_rows, rows(at, width)]
        sent([rcopy(ref, ref, ac_s, ac_r, mate)])

    def act_x():
        def piece(at, cols):
            return xf.at[pl.ds(pl.multiple_of(c * tokens + at * yrows, yrows), yrows), cols]

        for oy in [0] + order:
            at = yp(oy)
            ref = piece(at, own_cols)
            if oy:
                landing(ref, ay_r.at[at])()
            sent(rcopy(ref, ref, ax_s.at[0], ax_r.at[x], dev(z, y, c, xp(o))) for o in far(nx))
        ac(x)
        for o in range(1, nx):
            ref = xf.at[own_rows, rows(xp(o), width)]
            expect(("ax", o), landing(ref, ax_r.at[xp(o)]))
            left(ref, ax_s.at[0])

    def grad_z():
        z_step("oz", og_ref, zg, oz_s.at[0], oz_r.at[0])

    def grad_y():
        arrived("oz")
        sg[0] = swapped(zg[...])
        y_step("oy", sg.at[0], sg.at[1], 0, all_cols, oy_s.at[0], oy_r.at[0])
        sg[1, rows(y, yrows), :] = sg[0, rows(y, yrows), :]

    def act_c():
        for o in reversed(far(nx)):
            arrived(("ax", o))
            ac(xp(o))

    def grad_c():
        arrived("oy")
        sent([rcopy(sg.at[1, :, rows(1 - c, 2 * HDIM)], ogf.at[own_rows], oc_s, oc_r, mate)])
        left(ogf.at[own_rows], oc_s)
        expect("oc", landing(ogf.at[mate_rows], oc_r))
        ogf[own_rows, :] = sg[1, :, rows(c, 2 * HDIM)]

    def norm():
        left(xf.at[own_rows], ac_s)
        landing(xf.at[mate_rows], ac_r)()
        arrived("gains")
        square_sum = jnp.zeros((2 * tokens, 1), F32)
        for at in range(nx):
            act = xf[:, at * width:(at + 1) * width].astype(F32)
            square_sum += jnp.sum(act * act, axis=1, keepdims=True)
        inverse_rms = lax.rsqrt(square_sum / model + EPS)
        for at in range(nx):
            act = xf[:, at * width:(at + 1) * width].astype(F32)
            nrm[:, at * width:(at + 1) * width] = (act * inverse_rms * gains[at]).astype(BF16)
        state["inverse_rms"] = inverse_rms

    def grad_wait():
        arrived("oc")

    def project(h):
        proj = dot(nrm[...], ws[h][...])
        for p in range(2):
            state["proj", p, h] = of_position(proj, p)

    def attention(p):
        i = lax.broadcasted_iota(jnp.int32, (tokens, 1), 0)
        j = lax.broadcasted_iota(jnp.int32, (1, tokens), 1)

        def frame_of(r):
            return ((r & (nz - 1)) * ny + (lax.div(r, nz) & (ny - 1))) * 2 + lax.div(r, nz * ny)

        causal = frame_of(i) >= frame_of(j)
        scale = HDIM ** (-0.5)
        inner = jnp.zeros((tokens, 1), F32)
        for h in range(2):
            proj = state["proj", p, h]
            low = proj.astype(BF16)
            q, k, v = low[:, :HDIM], low[:, HDIM:2 * HDIM], low[:, 2 * HDIM:]
            g = of_position(ogf[:, h * HDIM:(h + 1) * HDIM].astype(F32), p).astype(BF16)
            scores = dot(q, k, NT) * scale
            exps = jnp.where(causal, jnp.exp(jnp.where(causal, scores, 0.0)), 0.0)
            probs = exps / jnp.sum(exps, axis=1, keepdims=True)
            dprobs = dot(g, v, NT)
            delta = jnp.sum(probs * dprobs, axis=1, keepdims=True)
            dscores = (probs * (dprobs - delta) * scale).astype(BF16)
            gq = dot(dscores, k).astype(BF16)
            gk = dot(dscores, q, TN).astype(BF16)
            gv = dot(probs.astype(BF16), g, TN).astype(BF16)
            for n, part_of in enumerate((gq, gk, gv)):
                gmix[p, h, :, n * HDIM:(n + 1) * HDIM] = part_of
                inner += jnp.sum(part_of.astype(F32) * proj[:, n * HDIM:(n + 1) * HDIM], axis=1, keepdims=True)
        state["inner", p] = inner / model

    xorder = tuple(far(nx)) + (0,)
    half = tokens // 2

    def combine(p, b):
        arrived(("pr", p, b))
        o = xorder[b]
        total = ig[p, b, rows(c, half), :] + part[p, b]
        if b < nx - 1:
            xsend[p, b] = total.astype(BF16)
            sems = xs_s.at[p, b], xs_r.at[p, b]
            sent([rcopy(xsend.at[p, b], xrecv.at[p, b], *sems, dev(z, y, c, xp(o)))])
            left(xsend.at[p, b], sems[0])
            expect(("xs", p, b), landing(xrecv.at[p, b], sems[1]))
        else:
            ig[p, b, rows(c, half), :] = total

    def backward(p):
        inner = state["inner", p]
        inverse_rms = of_position(state["inverse_rms"], p)
        for b, o in enumerate(xorder):
            at = xp(o)
            feats = rows(at, width)
            gn = dot(gmix[p, 0], w0[feats, :], NT) + dot(gmix[p, 1], w1[feats, :], NT)
            act = of_position(xf[:, feats].astype(F32), p) * inverse_rms
            terms = jnp.sum(gn * act, axis=0, keepdims=True)
            gsum[b] = gsum[b] + terms if p else terms
            ig[p, b] = inverse_rms * (gn * gains[at] - act * inner)
            sems = pr_s.at[p, b], pr_r.at[p, b]
            sent([rcopy(ig.at[p, b, rows(1 - c, half)], part.at[p, b], *sems, mate)])
            left(part.at[p, b], sems[0])
            expect(("pr", p, b), landing(part.at[p, b], sems[1]))
            if p and b > 0:
                combine(p, b - 1)

    def combine_first():
        for b in range(nx):
            combine(0, b)

    def combine_last():
        sent([rcopy(gsum, gpart, gp_s.at[0], gp_r.at[0], mate)])
        early, leaving[:] = leaving[:], []
        left(gsum, gp_s.at[0])
        combine(1, nx - 1)
        landing(gpart, gp_r.at[0])()
        gsend[...] = gsum[...] + gpart[...]
        gx[nx - 1] = gsend[nx - 1]
        sent(
            rcopy(gsend.at[b], gx.at[b], gx_s.at[0], gx_r.at[0], dev(z, y, c, xp(xorder[b]))) for b in range(nx - 1)
        )
        left(gsend.at[pl.ds(0, nx - 1)], gx_s.at[0])
        expect("gx", landing(gx.at[pl.ds(0, nx - 1)], gx_r.at[0]))
        for wait in early:
            wait()

    def back_y():
        totals = []
        for p in range(2):
            total = ig[p, nx - 1, rows(c, half), :]
            for b in range(nx - 1):
                arrived(("xs", p, b))
                total += xrecv[p, b].astype(F32)
            totals.append(total.reshape(ny, 1, nz, width))
        ysend[...] = jnp.concatenate(totals, axis=1).reshape(tokens, width).astype(BF16)
        y_step("by", ysend, yrecv, 0, all_cols, oy_s.at[1], oy_r.at[1])
        yrecv[rows(y, yrows), :] = ysend[rows(y, yrows), :]
        arrived("gx")
        gy[y] = jnp.sum(gx[...], axis=0)
        sent(rcopy(gy.at[y], gy.at[y], gy_s, gy_r, dev(z, yp(o), c, x)) for o in far(ny))
        left(gy.at[pl.ds(0, ny - 1)], gy_s)
        expect("gy", landing(gy.at[pl.ds(0, ny - 1)], gy_r))
        drain()

    def back_z():
        arrived("by")
        zsend[...] = swapped(yrecv[...], 1)
        z_step("bz", zsend, zrecv, oz_s.at[1], oz_r.at[1])
        zrecv[rows(z, zrows), :] = zsend[rows(z, zrows), :]
        arrived("gy")
        gz[z] = jnp.sum(gy[...], axis=0)
        sent(rcopy(gz.at[z], gz.at[z], gz_s, gz_r, dev(zp(o), y, c, x)) for o in far(nz))
        left(gz.at[pl.ds(0, nz - 1)], gz_s)
        expect("gz", landing(gz.at[pl.ds(0, nz - 1)], gz_r))

    def finish():
        arrived("bz")
        out_ref[...] = zrecv[...]
        arrived("gz")
        gg_ref[...] = jnp.sum(gz[...], axis=0).reshape(width)

    step = functools.partial
    stages = [
        begin, first_sends, weights_own, step(weights_0, order), act_y, step(hop, 1), act_x, grad_z,
        step(hop, 2), grad_y, step(hop, 3, (0,)), act_c, step(hop, 3, (1,)), grad_c, norm,
        step(last_hop, 0), step(project, 0), step(last_hop, 1), step(project, 1), grad_wait,
        step(attention, 0), step(backward, 0), combine_first, step(attention, 1), step(backward, 1), combine_last,
        back_y, back_z, finish,
    ]
    for stage in stages:
        stage()
    drain()


def shards(nz, ny, nx, activations, norm_gain, w_query, w_key, w_value, out_grad):
    tokens, width = activations.shape
    model = width * nx
    wcols = 3 * HDIM
    wrows = w_query.shape[0]
    vmem = pl.BlockSpec(memory_space=pltpu.VMEM)
    hbm = pl.BlockSpec(memory_space=pltpu.HBM)
    dma = pltpu.SemaphoreType.DMA
    ring = nz // 2
    scratch = [
        pltpu.VMEM((model, wcols), BF16),
        pltpu.VMEM((model, wcols), BF16),
        pltpu.VMEM((tokens, width), BF16),
        pltpu.VMEM((tokens, width), BF16),
        pltpu.VMEM((tokens, width), BF16),
        pltpu.VMEM((2, tokens, width), BF16),
        pltpu.VMEM((2 * tokens, model), BF16),
        pltpu.VMEM((2 * tokens, model), BF16),
        pltpu.VMEM((2 * tokens, 2 * HDIM), BF16),
        pltpu.VMEM((2, 2, tokens, wcols), BF16),
        pltpu.VMEM((nx, 1, width), F32),
        pltpu.VMEM((nx, 1, width), F32),
        pltpu.VMEM((nx, 1, width), F32),
        pltpu.VMEM((nx, 1, width), F32),
        pltpu.VMEM((ny, 1, width), F32),
        pltpu.VMEM((nz, 1, width), F32),
        pltpu.VMEM((nx, 1, width), F32),
        pltpu.VMEM((2, nx, tokens, width), F32),
        pltpu.VMEM((2, nx, tokens // 2, width), F32),
        pltpu.VMEM((2, nx, tokens // 2, width), BF16),
        pltpu.VMEM((2, nx, tokens // 2, width), BF16),
        pltpu.VMEM((tokens, width), BF16),
        pltpu.VMEM((tokens, width), BF16),
        pltpu.VMEM((tokens, width), BF16),
        pltpu.VMEM((tokens, width), BF16),
    ]
    scratch += [pltpu.VMEM((width,), BF16), pltpu.VMEM((2, tokens, tokens), BF16), dma((9,))]
    for shape in (
        (2,), (2, ny), (2, 2, ring, ny), (), (ny,), (nx,), (),
        (), (), (2, nx), (2, nx), (nx,), (nx,), (), (),
        (2,), (2,),
    ):
        scratch += [dma(shape), dma(shape)] if shape else [dma, dma]
    args = (activations, norm_gain, w_query, w_key, w_value, out_grad)
    args = tuple(pltpu.with_memory_space_constraint(arg, pltpu.HBM) for arg in args)
    return pl.pallas_call(
        functools.partial(kernel, nz, ny, nx),
        out_shape=(
            jax.ShapeDtypeStruct((tokens, width), BF16),
            jax.ShapeDtypeStruct((width,), F32),
        ),
        in_specs=[hbm] * 6,
        out_specs=(vmem, vmem),
        scratch_shapes=scratch,
        compiler_params=pltpu.CompilerParams(
            collective_id=0, has_side_effects=True, vmem_limit_bytes=24 * 1024 * 1024
        ),
    )(*args)


def solution(mesh, nz=8, ny=8):
    nx = mesh.shape["heads"]
    in_specs = (
        P("frames", "heads"),
        P("heads"),
        P("frames", "heads"),
        P("frames", "heads"),
        P("frames", "heads"),
        P("frames", "heads"),
    )
    out_specs = (P("frames", "heads"), P("heads"))
    return jax.shard_map(
        functools.partial(shards, nz, ny, nx),
        mesh=mesh, in_specs=in_specs, out_specs=out_specs, check_vma=False,
    )
```

```python
import functools

import jax
import jax.numpy as jnp
from jax import lax
from jax.experimental import pallas as pl
from jax.experimental.pallas import tpu as pltpu
from jax.sharding import PartitionSpec as P

EPS = 1e-05
HDIM = 128
F32 = jnp.float32
BF16 = jnp.bfloat16
NT = (((1,), (1,)), ((), ()))
TN = (((0,), (0,)), ((), ()))


def dot(a, b, dims=(((1,), (0,)), ((), ()))):
    return lax.dot_general(a, b, dims, preferred_element_type=F32)


def kernel(
    nz, ny, nx,
    a_ref, gain_ref, wq_ref, wk_ref, wv_ref, og_ref,
    out_ref, gg_ref,
    w0, w1, za, zg, sa, sg, xf, nrm, ogf, gmix,
    gains, gsum, gpart, gx, gy, gz, gsend, ig, part, xsend, xrecv, ysend, yrecv, zsend, zrecv,
    gain_low, hot, l_s, w_s, w_r, p1_s, p1_r, p2_s, p2_r, az_s, az_r, ay_s, ay_r, ax_s, ax_r, ac_s, ac_r,
    oc_s, oc_r, gn_s, gn_r, pr_s, pr_r, xs_s, xs_r, gp_s, gp_r, gx_s, gx_r, gy_s, gy_r, gz_s, gz_r,
    oy_s, oy_r, oz_s, oz_r,
):
    frame = lax.axis_index("frames")
    x = lax.axis_index("heads")
    c = frame & 1
    y = (frame >> 1) & (ny - 1)
    z = frame >> (ny.bit_length())
    chip = z * ny + y
    width = a_ref.shape[1]
    model = width * nx
    tokens = 2 * nz * ny
    zrows = 2 * ny
    yrows = 2 * nz
    wrows = wq_ref.shape[0]
    crows = 2 * wrows
    ws = (w0, w1)

    def dev(z_, y_, c_, x_):
        return ((z_ * ny + y_) * 2 + c_, x_)

    def rcopy(src, dst, ssem, rsem, to):
        return pltpu.make_async_remote_copy(
            src_ref=src, dst_ref=dst, send_sem=ssem, recv_sem=rsem,
            device_id=to, device_id_type=pl.DeviceIdType.MESH,
        )

    def wrap(v, n):
        return v & (n - 1)

    def rows(v, m):
        return pl.ds(pl.multiple_of(v * m, m), m)

    def block(zb, yb):
        return rows(zb * ny + yb, crows)

    mate = dev(z, y, 1 - c, x)
    own_rows, mate_rows = rows(c, tokens), rows(1 - c, tokens)
    own_cols, all_cols = rows(x, width), pl.ds(0, width)

    def yp(o):
        return wrap(y + o, ny)

    def zp(o):
        return wrap(z + o, nz)

    def xp(o):
        return wrap(x + o, nx)

    def far(n):
        return sorted(range(1, n), key=lambda o: -min(o, n - o))

    arriving, leaving, local = {}, [], []

    def sent(copies):
        for copy in copies:
            copy.start()

    def expect(name, *waits):
        arriving[name] = waits

    def arrived(name):
        for wait in arriving.pop(name):
            wait()

    def landing(ref, rsem):
        return lambda: rcopy(ref, ref, rsem, rsem, mate).wait_recv()

    def left(ref, ssem):
        leaving.append(lambda: rcopy(ref, ref, ssem, ssem, mate).wait_send())

    def z_step(name, src, dst, s, r):
        sent(
            rcopy(src.at[rows(zp(o), zrows)], dst.at[rows(z, zrows)], s, r, dev(zp(o), y, c, x))
            for o in far(nz)
        )
        bulk = dst.at[pl.ds(0, (nz - 1) * zrows)]
        left(bulk, s)
        expect(name, landing(bulk, r))

    def y_step(name, src, dst, base, cols, s, r, by_piece=False):
        def place(at):
            return dst.at[pl.ds(pl.multiple_of(base + at * yrows, yrows), yrows), cols]

        sent(
            rcopy(
                src.at[rows(yp(o), yrows)], place(y), s, r.at[y] if by_piece else r, dev(z, yp(o), c, x)
            )
            for o in far(ny)
        )
        bulk = src.at[pl.ds(0, (ny - 1) * yrows)]
        left(bulk, s)
        if not by_piece:
            expect(name, landing(bulk, r))

    def swap_rows(back):
        i = lax.broadcasted_iota(jnp.int32, (tokens, tokens), 1 if back else 0)
        j = lax.broadcasted_iota(jnp.int32, (tokens, tokens), 0 if back else 1)
        bits = nz.bit_length()
        source = (i & (nz - 1)) * zrows + (i >> bits) * 2 + ((i >> (bits - 1)) & 1)
        return jnp.where(j == source, 1.0, 0.0).astype(BF16)

    def swapped(value, back=0):
        return dot(hot[back], value).astype(BF16)

    def of_position(value, p):
        split = value.reshape(2 * ny, 2, nz, value.shape[1])
        return split[:, p].reshape(tokens, value.shape[1])

    def p1(j, o):
        ref = ws[j].at[block(z, y)]
        to = dev(z, yp(o), c, x) if j == 0 else dev(zp(o), y, c, x)
        return rcopy(ref, ref, p1_s.at[j, 0], p1_r.at[j, o], to)

    def p1_wait(j, o):
        landing(ws[j].at[block(z, yp(-o)) if j == 0 else block(zp(-o), y)], p1_r.at[j, o])()

    def place(j, d, age, k):
        sign = 1 if d == 0 else -1
        if j == 0:
            return ws[0].at[block(zp(-sign * age), wrap(y - k, ny))]
        return ws[1].at[block(wrap(z - k, nz), yp(-sign * age))]

    def p2(j, d, age, k):
        sign = 1 if d == 0 else -1
        to = dev(zp(sign), y, c, x) if j == 0 else dev(z, yp(sign), c, x)
        ref = place(j, d, age, k)
        return rcopy(ref, ref, p2_s.at[j, 0, 0, 0], p2_r.at[j, d, age, k], to)

    subs = ny
    last = nz // 2 - 1

    def goes(d, age, k):
        if age != last:
            return age < last
        return (k < subs // 2) if d == 0 else (k >= subs // 2)

    def each(act, halves=(0, 1)):
        for half in halves:
            for k in range(half * (subs // 2), (half + 1) * (subs // 2)):
                for j in range(2):
                    for d in range(2):
                        act(j, d, k, half * (subs - 1))

    def hop(age, halves=(0, 1)):
        def act(j, d, k, kind):
            if goes(d, age - 1, kind):
                landing(place(j, d, age, k), p2_r.at[j, d, age - 1, k])()
            if goes(d, age, kind):
                p2(j, d, age, k).start()

        each(act, halves)

    def last_hop(j):
        for k in range(subs):
            for d in range(2):
                if goes(d, last, k):
                    landing(place(j, d, last + 1, k), p2_r.at[j, d, last, k])()

    order = sorted(range(1, ny), key=lambda o: min(o, ny - o))

    def to_here(src, dst, n):
        copy = pltpu.make_async_copy(src, dst, l_s.at[n])
        copy.start()
        local.append(copy.wait)

    state = {}

    def drain():
        while leaving:
            leaving.pop(0)()

    def begin():
        peers = [mate]
        peers += [dev(z, yp(o), c, x) for o in range(1, ny)]
        peers += [dev(zp(o), y, c, x) for o in range(1, nz)]
        peers += [dev(z, y, c, xp(o)) for o in range(1, nx)]
        bar = pltpu.get_barrier_semaphore()
        for to in peers:
            pl.semaphore_signal(bar, inc=1, device_id=to, device_id_type=pl.DeviceIdType.MESH)

        for j in range(2):
            for i, w_ref in enumerate((wq_ref, wk_ref, wv_ref)):
                to_here(
                    w_ref.at[:, rows(2 * c + j, HDIM)],
                    ws[j].at[rows(2 * chip + c, wrows), i * HDIM:(i + 1) * HDIM],
                    3 * j + i,
                )
        to_here(a_ref.at[rows(z, zrows)], za.at[rows(z, zrows)], 6)
        to_here(og_ref.at[rows(z, zrows)], zg.at[rows(z, zrows)], 7)
        to_here(gain_ref, gain_low, 8)

        hot[0] = swap_rows(False)
        hot[1] = swap_rows(True)
        pl.semaphore_wait(bar, len(peers))

    def first_sends():
        for j in range(2):
            for i, w_ref in enumerate((wq_ref, wk_ref, wv_ref)):
                to = ws[j].at[rows(2 * chip + c, wrows), i * HDIM:(i + 1) * HDIM]
                sent([rcopy(w_ref.at[:, rows(2 * (1 - c) + j, HDIM)], to, w_s.at[j], w_r.at[j], mate)])
            ref = ws[j].at[rows(2 * chip + 1 - c, wrows)]
            left(ref, w_s.at[j])
            expect(("w", j), landing(ref, w_r.at[j]))
        z_step("az", a_ref, za, az_s, az_r)
        local.pop()()
        gains[x] = gain_low[...].astype(F32).reshape(1, width)
        sent(rcopy(gains.at[x], gains.at[x], gn_s, gn_r, dev(z, y, c, xp(o))) for o in far(nx))
        left(gains.at[pl.ds(0, nx - 1)], gn_s)
        expect("gains", landing(gains.at[pl.ds(0, nx - 1)], gn_r))

    def weights_own():
        for wait in local:
            wait()
        for j in range(2):
            arrived(("w", j))
            left(ws[j].at[pl.ds(0, (ny - 1) * crows)], p1_s.at[j, 0])
            count = sum(goes(d, age, k) for d in range(2) for age in range(last + 1) for k in range(subs))
            left(ws[j].at[pl.ds(0, count * crows)], p2_s.at[j, 0, 0, 0])
        for d in range(2):
            if goes(d, 0, 0):
                for j in range(2):
                    sent([p2(j, d, 0, 0)])
        for o in order:
            for j in range(2):
                sent([p1(j, o)])
        expect("p1", *(functools.partial(p1_wait, j, k) for k in order for j in range(2)))

    def act_y():
        arrived("az")
        sa[...] = swapped(za[...])
        y_step("ay", sa, xf, c * tokens, own_cols, ay_s.at[0], ay_r, True)
        xf[pl.ds(pl.multiple_of(c * tokens + y * yrows, yrows), yrows), own_cols] = sa[rows(y, yrows), :]

    def weights_0(ks):
        arriving.pop("p1", None)
        for k in ks:
            for j in range(2):
                p1_wait(j, k)
                for d in range(2):
                    if goes(d, 0, k):
                        sent([p2(j, d, 0, k)])

    def ac(at):
        ref = xf.at[own_rows, rows(at, width)]
        sent([rcopy(ref, ref, ac_s, ac_r, mate)])

    def act_x():
        def piece(at, cols):
            return xf.at[pl.ds(pl.multiple_of(c * tokens + at * yrows, yrows), yrows), cols]

        for oy in [0] + order:
            at = yp(oy)
            ref = piece(at, own_cols)
            if oy:
                landing(ref, ay_r.at[at])()
            sent(rcopy(ref, ref, ax_s.at[0], ax_r.at[x], dev(z, y, c, xp(o))) for o in far(nx))
        ac(x)
        for o in range(1, nx):
            ref = xf.at[own_rows, rows(xp(o), width)]
            expect(("ax", o), landing(ref, ax_r.at[xp(o)]))
            left(ref, ax_s.at[0])

    def grad_z():
        z_step("oz", og_ref, zg, oz_s.at[0], oz_r.at[0])

    def grad_y():
        arrived("oz")
        sg[0] = swapped(zg[...])
        y_step("oy", sg.at[0], sg.at[1], 0, all_cols, oy_s.at[0], oy_r.at[0])
        sg[1, rows(y, yrows), :] = sg[0, rows(y, yrows), :]

    def act_c():
        for o in reversed(far(nx)):
            arrived(("ax", o))
            ac(xp(o))

    def grad_c():
        arrived("oy")
        sent([rcopy(sg.at[1, :, rows(1 - c, 2 * HDIM)], ogf.at[own_rows], oc_s, oc_r, mate)])
        left(ogf.at[own_rows], oc_s)
        expect("oc", landing(ogf.at[mate_rows], oc_r))
        ogf[own_rows, :] = sg[1, :, rows(c, 2 * HDIM)]

    def norm():
        left(xf.at[own_rows], ac_s)
        landing(xf.at[mate_rows], ac_r)()
        arrived("gains")
        square_sum = jnp.zeros((2 * tokens, 1), F32)
        for at in range(nx):
            act = xf[:, at * width:(at + 1) * width].astype(F32)
            square_sum += jnp.sum(act * act, axis=1, keepdims=True)
        inverse_rms = lax.rsqrt(square_sum / model + EPS)
        for at in range(nx):
            act = xf[:, at * width:(at + 1) * width].astype(F32)
            nrm[:, at * width:(at + 1) * width] = (act * inverse_rms * gains[at]).astype(BF16)
        state["inverse_rms"] = inverse_rms

    def grad_wait():
        arrived("oc")

    def project(h):
        proj = dot(nrm[...], ws[h][...])
        for p in range(2):
            state["proj", p, h] = of_position(proj, p)

    def attention(p):
        i = lax.broadcasted_iota(jnp.int32, (tokens, 1), 0)
        j = lax.broadcasted_iota(jnp.int32, (1, tokens), 1)

        def frame_of(r):
            return ((r & (nz - 1)) * ny + (lax.div(r, nz) & (ny - 1))) * 2 + lax.div(r, nz * ny)

        causal = frame_of(i) >= frame_of(j)
        scale = HDIM ** (-0.5)
        inner = jnp.zeros((tokens, 1), F32)
        for h in range(2):
            proj = state["proj", p, h]
            low = proj.astype(BF16)
            q, k, v = low[:, :HDIM], low[:, HDIM:2 * HDIM], low[:, 2 * HDIM:]
            g = of_position(ogf[:, h * HDIM:(h + 1) * HDIM].astype(F32), p).astype(BF16)
            scores = dot(q, k, NT) * scale
            exps = jnp.where(causal, jnp.exp(jnp.where(causal, scores, 0.0)), 0.0)
            probs = exps / jnp.sum(exps, axis=1, keepdims=True)
            dprobs = dot(g, v, NT)
            delta = jnp.sum(probs * dprobs, axis=1, keepdims=True)
            dscores = (probs * (dprobs - delta) * scale).astype(BF16)
            gq = dot(dscores, k).astype(BF16)
            gk = dot(dscores, q, TN).astype(BF16)
            gv = dot(probs.astype(BF16), g, TN).astype(BF16)
            for n, part_of in enumerate((gq, gk, gv)):
                gmix[p, h, :, n * HDIM:(n + 1) * HDIM] = part_of
                inner += jnp.sum(part_of.astype(F32) * proj[:, n * HDIM:(n + 1) * HDIM], axis=1, keepdims=True)
        state["inner", p] = inner / model

    xorder = tuple(far(nx)) + (0,)
    half = tokens // 2

    def combine(p, b):
        arrived(("pr", p, b))
        o = xorder[b]
        total = ig[p, b, rows(c, half), :] + part[p, b]
        if b < nx - 1:
            xsend[p, b] = total.astype(BF16)
            sems = xs_s.at[p, b], xs_r.at[p, b]
            sent([rcopy(xsend.at[p, b], xrecv.at[p, b], *sems, dev(z, y, c, xp(o)))])
            left(xsend.at[p, b], sems[0])
            expect(("xs", p, b), landing(xrecv.at[p, b], sems[1]))
        else:
            ig[p, b, rows(c, half), :] = total

    def backward(p):
        inner = state["inner", p]
        inverse_rms = of_position(state["inverse_rms"], p)
        for b, o in enumerate(xorder):
            at = xp(o)
            feats = rows(at, width)
            gn = dot(gmix[p, 0], w0[feats, :], NT) + dot(gmix[p, 1], w1[feats, :], NT)
            act = of_position(xf[:, feats].astype(F32), p) * inverse_rms
            terms = jnp.sum(gn * act, axis=0, keepdims=True)
            gsum[b] = gsum[b] + terms if p else terms
            ig[p, b] = inverse_rms * (gn * gains[at] - act * inner)
            sems = pr_s.at[p, b], pr_r.at[p, b]
            sent([rcopy(ig.at[p, b, rows(1 - c, half)], part.at[p, b], *sems, mate)])
            left(part.at[p, b], sems[0])
            expect(("pr", p, b), landing(part.at[p, b], sems[1]))
            if p and b > 0:
                combine(p, b - 1)

    def combine_first():
        for b in range(nx):
            combine(0, b)

    def combine_last():
        sent([rcopy(gsum, gpart, gp_s.at[0], gp_r.at[0], mate)])
        early, leaving[:] = leaving[:], []
        left(gsum, gp_s.at[0])
        combine(1, nx - 1)
        landing(gpart, gp_r.at[0])()
        gsend[...] = gsum[...] + gpart[...]
        gx[nx - 1] = gsend[nx - 1]
        sent(
            rcopy(gsend.at[b], gx.at[b], gx_s.at[0], gx_r.at[0], dev(z, y, c, xp(xorder[b]))) for b in range(nx - 1)
        )
        left(gsend.at[pl.ds(0, nx - 1)], gx_s.at[0])
        expect("gx", landing(gx.at[pl.ds(0, nx - 1)], gx_r.at[0]))
        for wait in early:
            wait()

    def back_y():
        totals = []
        for p in range(2):
            total = ig[p, nx - 1, rows(c, half), :]
            for b in range(nx - 1):
                arrived(("xs", p, b))
                total += xrecv[p, b].astype(F32)
            totals.append(total.reshape(ny, 1, nz, width))
        ysend[...] = jnp.concatenate(totals, axis=1).reshape(tokens, width).astype(BF16)
        y_step("by", ysend, yrecv, 0, all_cols, oy_s.at[1], oy_r.at[1])
        yrecv[rows(y, yrows), :] = ysend[rows(y, yrows), :]
        arrived("gx")
        gy[y] = jnp.sum(gx[...], axis=0)
        sent(rcopy(gy.at[y], gy.at[y], gy_s, gy_r, dev(z, yp(o), c, x)) for o in far(ny))
        left(gy.at[pl.ds(0, ny - 1)], gy_s)
        expect("gy", landing(gy.at[pl.ds(0, ny - 1)], gy_r))
        drain()

    def back_z():
        arrived("by")
        zsend[...] = swapped(yrecv[...], 1)
        z_step("bz", zsend, zrecv, oz_s.at[1], oz_r.at[1])
        zrecv[rows(z, zrows), :] = zsend[rows(z, zrows), :]
        arrived("gy")
        gz[z] = jnp.sum(gy[...], axis=0)
        sent(rcopy(gz.at[z], gz.at[z], gz_s, gz_r, dev(zp(o), y, c, x)) for o in far(nz))
        left(gz.at[pl.ds(0, nz - 1)], gz_s)
        expect("gz", landing(gz.at[pl.ds(0, nz - 1)], gz_r))

    def finish():
        arrived("bz")
        out_ref[...] = zrecv[...]
        arrived("gz")
        gg_ref[...] = jnp.sum(gz[...], axis=0).reshape(width)

    step = functools.partial
    stages = [
        begin, first_sends, weights_own, step(weights_0, order), act_y, step(hop, 1), act_x, grad_z,
        step(hop, 2), grad_y, step(hop, 3, (0,)), act_c, step(hop, 3, (1,)), grad_c, norm,
        step(last_hop, 0), step(project, 0), step(last_hop, 1), step(project, 1), grad_wait,
        step(attention, 0), step(backward, 0), combine_first, step(attention, 1), step(backward, 1), combine_last,
        back_y, back_z, finish,
    ]
    for stage in stages:
        stage()
    drain()


def shards(nz, ny, nx, activations, norm_gain, w_query, w_key, w_value, out_grad):
    tokens, width = activations.shape
    model = width * nx
    wcols = 3 * HDIM
    wrows = w_query.shape[0]
    vmem = pl.BlockSpec(memory_space=pltpu.VMEM)
    hbm = pl.BlockSpec(memory_space=pltpu.HBM)
    dma = pltpu.SemaphoreType.DMA
    ring = nz // 2
    scratch = [
        pltpu.VMEM((model, wcols), BF16),
        pltpu.VMEM((model, wcols), BF16),
        pltpu.VMEM((tokens, width), BF16),
        pltpu.VMEM((tokens, width), BF16),
        pltpu.VMEM((tokens, width), BF16),
        pltpu.VMEM((2, tokens, width), BF16),
        pltpu.VMEM((2 * tokens, model), BF16),
        pltpu.VMEM((2 * tokens, model), BF16),
        pltpu.VMEM((2 * tokens, 2 * HDIM), BF16),
        pltpu.VMEM((2, 2, tokens, wcols), BF16),
        pltpu.VMEM((nx, 1, width), F32),
        pltpu.VMEM((nx, 1, width), F32),
        pltpu.VMEM((nx, 1, width), F32),
        pltpu.VMEM((nx, 1, width), F32),
        pltpu.VMEM((ny, 1, width), F32),
        pltpu.VMEM((nz, 1, width), F32),
        pltpu.VMEM((nx, 1, width), F32),
        pltpu.VMEM((2, nx, tokens, width), F32),
        pltpu.VMEM((2, nx, tokens // 2, width), F32),
        pltpu.VMEM((2, nx, tokens // 2, width), BF16),
        pltpu.VMEM((2, nx, tokens // 2, width), BF16),
        pltpu.VMEM((tokens, width), BF16),
        pltpu.VMEM((tokens, width), BF16),
        pltpu.VMEM((tokens, width), BF16),
        pltpu.VMEM((tokens, width), BF16),
    ]
    scratch += [pltpu.VMEM((width,), BF16), pltpu.VMEM((2, tokens, tokens), BF16), dma((9,))]
    for shape in (
        (2,), (2, ny), (2, 2, ring, ny), (), (ny,), (nx,), (),
        (), (), (2, nx), (2, nx), (nx,), (nx,), (), (),
        (2,), (2,),
    ):
        scratch += [dma(shape), dma(shape)] if shape else [dma, dma]
    args = (activations, norm_gain, w_query, w_key, w_value, out_grad)
    args = tuple(pltpu.with_memory_space_constraint(arg, pltpu.HBM) for arg in args)
    return pl.pallas_call(
        functools.partial(kernel, nz, ny, nx),
        out_shape=(
            jax.ShapeDtypeStruct((tokens, width), BF16),
            jax.ShapeDtypeStruct((width,), F32),
        ),
        in_specs=[hbm] * 6,
        out_specs=(vmem, vmem),
        scratch_shapes=scratch,
        compiler_params=pltpu.CompilerParams(
            collective_id=0, has_side_effects=True, vmem_limit_bytes=24 * 1024 * 1024
        ),
    )(*args)


def solution(mesh, nz=8, ny=8):
    nx = mesh.shape["heads"]
    in_specs = (
        P("frames", "heads"),
        P("heads"),
        P("frames", "heads"),
        P("frames", "heads"),
        P("frames", "heads"),
        P("frames", "heads"),
    )
    out_specs = (P("frames", "heads"), P("heads"))
    return jax.shard_map(
        functools.partial(shards, nz, ny, nx),
        mesh=mesh, in_specs=in_specs, out_specs=out_specs, check_vma=False,
    )
```
